128 devices in a mesh: dom: 32 (over z, y, core), head: 4 (over x).
Axes of the slice: x: 4, y: 4, z: 4, core: 2. Of those that a mesh axis runs over, the one named last changes fastest.
Arguments:
- features: bfloat16 [131072, 128], P('dom'), may hold values from -20 to 20
- qkv_weight: bfloat16 [128, 3, 128], P(None, None, 'head'), may hold values from -0.5 to 0.5
- out_weight: bfloat16 [128, 128], replicated, may hold values from -0.5 to 0.5
- ffn_in: bfloat16 [128, 256], P(None, 'head'), may hold values from -0.5 to 0.5
- ffn_out: bfloat16 [256, 128], P('head'), may hold values from -0.375 to 0.375
- norm_gains: float32 [2, 128], replicated, may hold values from 0.25 to 1.75
- virtual_table: bfloat16 [8, 128], replicated, may hold values from -6 to 6
- block_mask: int32 [131072, 128], P('dom'), may hold values 0 or 1
- halo_send: int32 [32, 2, 2048], P('dom'), may hold values from 0 to 4095
- halo_links: int32 [131072, 4], P('dom'), may hold values from 0 to 4095
- expander_perm: int32 [3, 32, 4096], P(None, 'dom'), may hold values from 0 to 4095, each once within a row
- virtual_ids: int32 [131072], P('dom'), may hold values from 0 to 7
Outputs:
- layer_out: bfloat16 [131072, 128], P(('dom', 'head'))
The draws below stay inside these ranges and needn't reach their ends.
All inputs are finite; a program needn't handle non-finite values. No bound on the sum of `block_mask` on one device may be relied on, other than what follows from the above.
Results may differ from the reference program's by a relative error of at most 0.015.
Values may be sent and summed in bfloat16 or wider, within the bound.
A program may use at most 64 MiB of HBM per device.

```python
import math
import jax
import jax.numpy as jnp
import numpy as np
from jax import lax

D = 128
HEAD_DIM = 16
FF = 256
VIRT = 8
BLOCK = 128
HDEG = 4
NODE_DEV = 4096
HALO = 2048
NODES = 131072
N_DOM = 32


def draw_features(key, part):
    key = jax.random.fold_in(key, 11)
    first_key = jax.random.fold_in(key, 0)
    drawn = jax.random.normal(first_key, (NODES, D), jnp.float32)
    return jnp.clip(drawn, -20.0, 20.0).astype(jnp.bfloat16)


def place_ends(array, stream_key, smallest, top_value):
    index_at = [jax.random.randint(jax.random.fold_in(stream_key, axis), (), 0, length) for axis, length in enumerate(array.shape)]
    longest = array.shape.index(max(array.shape))
    beside = index_at[:longest] + [(index_at[longest] + 1) % array.shape[longest]] + index_at[longest + 1:]
    return array.at[tuple(index_at)].set(smallest).at[tuple(beside)].set(top_value)


def block_scale(stream_key, extent, cuts, smallest, high):
    loudness, own = 1.0, jax.random.fold_in(stream_key, 6)
    for dim, shards_of in cuts:
        heights = jnp.exp(jax.random.uniform(jax.random.fold_in(own, dim), (shards_of,), jnp.float32, smallest / len(cuts), high / len(cuts)))
        loudness = loudness * jnp.repeat(heights, extent[dim] // shards_of).reshape([-1 if axis == dim else 1 for axis in range(len(extent))])
    return loudness


def cumulative_ranks(amount, skew):
    weights = [(1 << 20) // math.isqrt(rank ** skew) + 1 for rank in range(1, amount + 1)]
    width = 1 + sum(weights) // (1 << 30)
    return np.cumsum(np.array([max(1, weight // width) for weight in weights]))


def ranked_ids(key, dims, count, skew):
    table = cumulative_ranks(count, skew)
    lot = jax.random.randint(jax.random.fold_in(key, 1), dims, 0, int(table[count - 1]))
    standing = jnp.searchsorted(jnp.asarray(table, jnp.int32), lot, side="right")
    return jax.random.permutation(jax.random.fold_in(key, 2), count)[standing].astype(jnp.int32)


def centred(own_key, extent, width, most, cuts=(), held_as=jnp.bfloat16):
    level = block_scale(own_key, extent, cuts, -0.22, 0.18) if cuts else 1.0
    values = jax.random.normal(own_key, extent, jnp.float32) * width * level
    return jnp.minimum(jnp.maximum(values, -most), most).astype(held_as)


def setup_inputs(seed: int = 0) -> dict:
    streams_of = jax.random.split(jax.random.key(seed), 13)
    return {
        "features": draw_features(jax.random.fold_in(streams_of[12], 71), 0),
        "qkv_weight": centred(streams_of[1], (D, 3, D), D ** -0.5, 0.5, ((2, 4),)),
        "out_weight": centred(streams_of[2], (D, D), D ** -0.5, 0.5),
        "ffn_in": centred(streams_of[3], (D, FF), D ** -0.5, 0.5, ((1, 4),)),
        "ffn_out": centred(streams_of[4], (FF, D), FF ** -0.5, 0.375, ((0, 4),)),
        "norm_gains": jnp.clip(1.0 + 0.15 * jax.random.normal(streams_of[5], (2, D), jnp.float32), 0.25, 1.75),
        "virtual_table": centred(streams_of[6], (VIRT, D), 1.0, 6.0),
        "block_mask": place_ends((jax.random.randint(streams_of[7], (NODES, BLOCK), 0, 4) < 1).astype(jnp.int32), jax.random.fold_in(streams_of[7], 1), 0, 1),
        "halo_send": place_ends(jax.random.randint(streams_of[8], (N_DOM, 2, HALO), 0, NODE_DEV), jax.random.fold_in(streams_of[8], 1), 0, NODE_DEV - 1).astype(jnp.int32),
        "halo_links": place_ends(jax.random.randint(streams_of[9], (NODES, HDEG), 0, 2 * HALO), jax.random.fold_in(streams_of[9], 1), 0, (2 * HALO) - 1).astype(jnp.int32),
        "expander_perm": jax.vmap(lambda own: jax.random.permutation(own, NODE_DEV))(jax.random.split(streams_of[10], 3 * N_DOM)).reshape((3, N_DOM, NODE_DEV)).astype(jnp.int32),
        "virtual_ids": place_ends(ranked_ids(streams_of[11], (NODES,), VIRT, 2), jax.random.fold_in(streams_of[11], 3), 0, VIRT - 1).astype(jnp.int32),
    }


def layer_norm(values_in, gain):
    center = lax.optimization_barrier(jnp.mean(values_in, axis=-1, keepdims=True))
    shifted = values_in - center
    second = lax.optimization_barrier(jnp.mean(shifted * shifted, axis=-1, keepdims=True))
    return shifted * lax.rsqrt(second + 1e-05) * gain

def attend(queries, key_rows, value_rows, allowed, extra_keys, extra_values):
    node_count, model_width = queries.shape
    head_count = model_width // HEAD_DIM
    block_count = node_count // BLOCK
    q_blocks = queries.astype(jnp.float32).reshape(block_count, BLOCK, head_count, HEAD_DIM)
    k_blocks = key_rows.astype(jnp.float32).reshape(block_count, BLOCK, head_count, HEAD_DIM)
    v_blocks = value_rows.astype(jnp.float32).reshape(block_count, BLOCK, head_count, HEAD_DIM)
    near_scores = jnp.einsum('bihd,bjhd->bihj', q_blocks, k_blocks) * HEAD_DIM ** (-0.5)
    near_scores = near_scores.reshape(node_count, head_count, BLOCK)
    extra_count = extra_keys.shape[1]
    far_keys = extra_keys.astype(jnp.float32).reshape(node_count, extra_count, head_count, HEAD_DIM)
    far_values = extra_values.astype(jnp.float32).reshape(node_count, extra_count, head_count, HEAD_DIM)
    q_nodes = queries.astype(jnp.float32).reshape(node_count, head_count, HEAD_DIM)
    far_scores = jnp.einsum('nhd,nehd->nhe', q_nodes, far_keys) * HEAD_DIM ** (-0.5)
    scores = jnp.concatenate([jnp.where(allowed[:, None, :], near_scores, -1e+30), far_scores], axis=-1)
    row_max = lax.optimization_barrier(jnp.max(scores, axis=-1, keepdims=True))
    exponent = jnp.exp(scores - row_max)
    row_total = lax.optimization_barrier(jnp.sum(exponent, axis=-1, keepdims=True))
    weights = (exponent / row_total).astype(jnp.bfloat16).astype(jnp.float32)
    near_weights = weights[..., :BLOCK].reshape(block_count, BLOCK, head_count, BLOCK)
    combined = jnp.einsum('bihj,bjhd->bihd', near_weights, v_blocks).reshape(node_count, head_count, HEAD_DIM)
    combined = combined + jnp.einsum('nhe,nehd->nhd', weights[..., BLOCK:], far_values)
    return combined.reshape(node_count, model_width).astype(jnp.bfloat16)

def reference(features, qkv_weight, out_weight, ffn_in, ffn_out, norm_gains, virtual_table, block_mask, halo_send, halo_links, expander_perm, virtual_ids):
    projected = jnp.dot(features, qkv_weight.reshape(D, 3 * D), preferred_element_type=jnp.float32).astype(jnp.bfloat16)
    projected = projected.reshape(NODES, 3, D)
    queries = projected[:, 0].reshape(N_DOM, NODE_DEV, D)
    key_value = jnp.concatenate([projected[:, 1], projected[:, 2]], axis=1).reshape(N_DOM, NODE_DEV, 2 * D)
    virtual_kv = jnp.dot(virtual_table, qkv_weight[:, 1:].reshape(D, 2 * D), preferred_element_type=jnp.float32).astype(jnp.bfloat16)
    virtual_kv = virtual_kv.reshape(VIRT, 2, D).reshape(VIRT, 2 * D)
    levels = N_DOM.bit_length() - 1
    shifts = [matching * (levels - 1) // 2 for matching in range(3)]
    mask_parts = block_mask.reshape(N_DOM, NODE_DEV, BLOCK)
    link_parts = halo_links.reshape(N_DOM, NODE_DEV, HDEG)
    id_parts = virtual_ids.reshape(N_DOM, NODE_DEV)
    position = jnp.arange(NODE_DEV, dtype=jnp.int32) % BLOCK
    diagonal = position[:, None] == jnp.arange(BLOCK, dtype=jnp.int32)[None, :]

    def one_part(index):
        lower = (index - 1) % N_DOM
        upper = (index + 1) % N_DOM
        from_below = key_value[lower][halo_send[lower, 1]]
        from_above = key_value[upper][halo_send[upper, 0]]
        halo_rows = jnp.concatenate([from_below, from_above], axis=0)
        linked = halo_rows[link_parts[index]]
        partner_list = []
        for matching in range(3):
            partner = jnp.bitwise_xor(index, jnp.int32(1 << shifts[matching]))
            partner_list.append(key_value[partner][expander_perm[matching, index]])
        paired = jnp.stack(partner_list, axis=1)
        hub_rows = virtual_kv[id_parts[index]]
        extra_rows = jnp.concatenate([linked, paired, hub_rows[:, None, :]], axis=1)
        allowed = (mask_parts[index] > 0) | diagonal
        own_kv = key_value[index]
        return attend(queries[index], own_kv[:, :D], own_kv[:, D:], allowed, extra_rows[..., :D], extra_rows[..., D:])
    attended = lax.map(one_part, jnp.arange(N_DOM, dtype=jnp.int32)).reshape(NODES, D)
    mixed_out = jnp.dot(attended, out_weight, preferred_element_type=jnp.float32)
    hidden_in = layer_norm(features.astype(jnp.float32) + mixed_out, norm_gains[0]).astype(jnp.bfloat16)
    inner = jax.nn.gelu(jnp.dot(hidden_in, ffn_in, preferred_element_type=jnp.float32), approximate=True).astype(jnp.bfloat16)
    summed = jnp.dot(inner, ffn_out, preferred_element_type=jnp.float32)
    return layer_norm(hidden_in.astype(jnp.float32) + summed, norm_gains[1]).astype(jnp.bfloat16)
```

```python
import functools

import jax
import jax.numpy as jnp
from jax import lax
from jax.experimental import pallas as pl
from jax.experimental.pallas import tpu as pltpu
from jax.sharding import PartitionSpec as P

HEAD_DIM = 16
BLOCK = 128
ROWS = 64
MESH = pl.DeviceIdType.MESH
F32 = jnp.float32
BF16 = jnp.bfloat16


def dot_nt(a, b):
    return lax.dot_general(a, b, (((1,), (1,)), ((), ())), preferred_element_type=F32)


def dot_nn(a, b):
    return jnp.dot(a, b, preferred_element_type=F32)


def gather_rows(count, index_of, table, out, out_base):
    def step(i, carry):
        base = pl.multiple_of(i * ROWS, ROWS)
        for u in range(ROWS):
            out[pl.ds(out_base + base + u, 1), :] = table[pl.ds(index_of(base + u), 1), :]
        return carry

    lax.fori_loop(0, count // ROWS, step, 0)


def widen(source, out, out_base, rows):
    def step(i, carry):
        at = pl.multiple_of(i * 256, 256)
        out[pl.ds(pl.multiple_of(out_base + at, 256), 256), :] = source[pl.ds(at, 256), :].astype(F32)
        return carry

    lax.fori_loop(0, rows // 256, step, 0)


def exchange_kernel(
    n_dom,
    n_head,
    feats,
    send_smem,
    send_vmem,
    perm,
    wqkv,
    w1,
    w2,
    peer_feats,
    near_list,
    rows_a,
    rows_b,
    lookup,
    weights,
    table,
    staged,
    packed,
    wpack,
    peer_send,
    request,
    request_smem,
    feats_sems,
    send_sems,
    req_send,
    req_recv,
    list_send,
    list_recv,
    rows_send,
    rows_recv,
    w_send,
    w_recv,
    local_sem,
):
    nodes = feats.shape[0]
    halo = near_list.shape[0]
    part = rows_a.shape[0]
    dom = lax.axis_index("dom")
    head = lax.axis_index("head")
    core = lax.rem(dom, 2)
    peer = dom + 1 - 2 * core
    side = lax.rem(dom + 2 * core - 1 + n_dom, n_dom)
    levels = n_dom.bit_length() - 1

    def flipped(stride):
        bit = lax.rem(dom // (1 << stride), 2)
        return dom + (1 - 2 * bit) * (1 << stride)

    partners = [flipped(m * (levels - 1) // 2) for m in (1, 2)]
    others = [lax.rem(head + k, n_head) for k in range(1, n_head)]

    barrier = pltpu.get_barrier_semaphore()
    for dev in [peer, side] + partners:
        pl.semaphore_signal(barrier, inc=1, device_id={"dom": dev}, device_id_type=MESH)
    for dev in others:
        pl.semaphore_signal(barrier, inc=1, device_id={"head": dev}, device_id_type=MESH)
    pl.semaphore_wait(barrier, 4 + len(others))

    def remote(src, dst, send, recv, device):
        return pltpu.make_async_remote_copy(
            src_ref=src, dst_ref=dst, send_sem=send, recv_sem=recv, device_id=device, device_id_type=MESH
        )

    started = []
    for m in (0, 1):
        copy = remote(
            perm.at[m + 1, 0, pl.ds(pl.multiple_of(head * part, 128), part)],
            request.at[m],
            req_send.at[m],
            req_recv.at[m],
            {"dom": partners[m]},
        )
        copy.start()
        started.append(copy)
    requests = list(started)
    send_copy = remote(send_vmem, peer_send, send_sems.at[0], send_sems.at[1], {"dom": peer})
    send_copy.start()
    feats_copy = remote(feats, peer_feats, feats_sems.at[0], feats_sems.at[1], {"dom": peer})
    feats_copy.start()

    q_rows, f_rows = wqkv.shape[0], w1.shape[0]
    wpack[0:q_rows, :] = wqkv[...]
    wpack[q_rows : q_rows + f_rows, :] = w1[...]
    wpack[q_rows + f_rows : q_rows + 2 * f_rows, :] = w2[...]
    w_copies = []
    for k, dev in enumerate(others):
        copy = remote(wpack, weights.at[head], w_send.at[k], w_recv.at[head], {"head": dev})
        copy.start()
        w_copies.append(copy)
    own = pltpu.make_async_copy(wpack, weights.at[head], local_sem.at[0])
    own.start()

    widen(feats, table, 0, nodes)

    chunk = staged.shape[0]

    def send_chunk(index_of, at, slot, dst, send, recv, device):
        gather_rows(chunk, index_of, table, staged, 0)
        packed[slot] = staged[...].astype(BF16)
        copy = remote(packed.at[slot], dst.at[pl.ds(at, chunk), :], send, recv, device)
        copy.start()
        return copy

    chunks = []
    slot = 0
    for i in range(halo // chunk):
        chunks.append(
            send_chunk(
                lambda r, i=i: send_smem[core, i * chunk + r],
                i * chunk,
                slot,
                near_list,
                list_send.at[i],
                list_recv.at[i],
                {"dom": side},
            )
        )
        slot += 1
    for m, dst in ((0, rows_a), (1, rows_b)):
        requests[m].wait_recv()
        moved = pltpu.make_async_copy(request.at[m], request_smem.at[m], local_sem.at[1 + m])
        moved.start()
        moved.wait()
        for i in range(part // chunk):
            k = m * (part // chunk) + i
            chunks.append(
                send_chunk(
                    lambda r, i=i, m=m: request_smem[m, i * chunk + r],
                    i * chunk,
                    slot,
                    dst,
                    rows_send.at[k],
                    rows_recv.at[k],
                    {"dom": partners[m]},
                )
            )
            slot += 1

    send_copy.wait()
    ramp = nodes + lax.broadcasted_iota(jnp.int32, (1, halo), 1)
    even = core == 0
    lookup[0:1, :] = jnp.where(even, ramp, peer_send[1:2, :])
    lookup[1:2, :] = jnp.where(even, peer_send[0:1, :], ramp)

    for copy in requests:
        copy.wait_send()
    feats_copy.wait()
    own.wait()
    for k, copy in enumerate(w_copies):
        copy.wait_send()
    for dev in others:
        remote(wpack, weights.at[dev], w_send.at[0], w_recv.at[dev], {"head": dev}).wait_recv()
    for copy in chunks:
        copy.wait()


def layer_norm_cols(values, gain):
    count = values.shape[0]
    center = jnp.sum(values, axis=0, keepdims=True) * (1.0 / count)
    shifted = values - center
    second = jnp.sum(shifted * shifted, axis=0, keepdims=True) * (1.0 / count)
    return shifted * lax.rsqrt(second + 1e-05) * gain


def layer_kernel(
    at_head,
    links,
    perm,
    lookup,
    peer_feats,
    near_list,
    rows_a,
    rows_b,
    feats,
    mask,
    vids,
    vtab,
    weights,
    wo,
    gains,
    out,
    table,
    far,
    q_t,
    q_rows,
    k_rows,
    v_t,
    far_w,
):
    del at_head
    nodes, width = feats.shape
    n_head = weights.shape[0]
    local = width // n_head
    heads = width // HEAD_DIM
    link_count = links.shape[0]
    n_virt = vtab.shape[0]
    f_rows = (weights.shape[1] - 3 * local) // 2

    def gathered(lo, count):
        return jnp.concatenate([weights[h, lo : lo + count, :] for h in range(n_head)], axis=0)

    wq_t = gathered(0, local)
    wk_t = gathered(local, local)
    wv_t = gathered(2 * local, local)
    w1_t = gathered(3 * local, f_rows)
    eye = (
        lax.broadcasted_iota(jnp.int32, (width, width), 0)
        == lax.broadcasted_iota(jnp.int32, (width, width), 1)
    ).astype(BF16)
    w2_t = dot_nt(eye, gathered(3 * local + f_rows, f_rows)).astype(BF16)
    wo_t = dot_nt(eye, wo[...]).astype(BF16)
    gain_cols = [
        jnp.transpose(jnp.broadcast_to(gains[g : g + 1, :], (width, width))) for g in (0, 1)
    ]
    far_w[...] = jnp.concatenate([wk_t, wv_t], axis=0)
    far_t = far_w[...]

    widen(peer_feats, table, 0, peer_feats.shape[0])
    widen(near_list, table, peer_feats.shape[0], near_list.shape[0])
    for e in range(link_count):
        gather_rows(nodes, lambda r, e=e: lookup[links[e, r]], table, far, e * nodes)
    gather_rows(nodes, lambda r: perm[0, 0, r], table, far, link_count * nodes)

    scale = HEAD_DIM ** (-0.5)
    own = feats[...]
    q_rows[...] = (dot_nt(own, wq_t).astype(BF16) * scale).astype(BF16)
    k_rows[...] = dot_nt(own, wk_t).astype(BF16)
    q_t[...] = (dot_nt(wq_t, own).astype(BF16) * scale).astype(F32)
    v_t[...] = dot_nt(wv_t, own).astype(BF16)
    vk = dot_nt(vtab[...], wk_t).astype(BF16)
    vv_t = dot_nt(wv_t, vtab[...]).astype(BF16)

    lane_head = lax.broadcasted_iota(jnp.int32, (BLOCK, width), 1) // HEAD_DIM
    sub_head = lax.broadcasted_iota(jnp.int32, (width, BLOCK), 0) // HEAD_DIM
    zero = jnp.zeros((), BF16)

    def by_head_rows(rows):
        lanes = lane_head[0 : rows.shape[0]]
        return jnp.concatenate([jnp.where(lanes == h, rows, zero) for h in range(heads)], axis=0)

    def by_head_cols(cols):
        subs = lax.broadcasted_iota(jnp.int32, cols.shape, 0) // HEAD_DIM
        return jnp.concatenate([jnp.where(subs == h, cols, zero) for h in range(heads)], axis=1)

    vk_heads = by_head_rows(vk)
    vv_heads = by_head_cols(vv_t)
    eyes = jnp.concatenate([eye] * heads, axis=0)
    diag = lax.broadcasted_iota(jnp.int32, (BLOCK, BLOCK), 0) == lax.broadcasted_iota(
        jnp.int32, (BLOCK, BLOCK), 1
    )

    def expand(per_head):
        return jnp.broadcast_to(
            per_head[:, None, :], (heads, HEAD_DIM, per_head.shape[-1])
        ).reshape(width, per_head.shape[-1])

    def step(b, carry):
        at = pl.multiple_of(b * BLOCK, BLOCK)
        here = pl.ds(at, BLOCK)
        feat = feats[here, :]
        k_heads = jnp.concatenate([by_head_rows(k_rows[here, :]), eyes], axis=1)
        allowed = (mask[here, :] > 0) | diag
        bias = jnp.where(allowed, 0.0, -1e30).astype(BF16)
        near = dot_nt(k_heads, jnp.concatenate([q_rows[here, :], bias], axis=1))
        near = near.reshape(heads, BLOCK, BLOCK)
        hub = dot_nt(vk_heads, q_rows[here, :]).reshape(heads, n_virt, BLOCK)
        mine = vids[0:1, here] == lax.broadcasted_iota(jnp.int32, (n_virt, BLOCK), 0)
        hub = jnp.where(mine[None], hub, -1e30)
        queries = q_t[:, here]
        far_scores = []
        far_values = []
        for e in range(link_count + 3):
            if e <= link_count:
                rows = far[pl.ds(pl.multiple_of(e * nodes + at, BLOCK), BLOCK), :].astype(BF16)
            else:
                rows = (rows_a if e == link_count + 1 else rows_b)[here, :]
            kv = dot_nt(far_t, rows).astype(BF16).astype(F32)
            prod = (kv[0:width] * queries).reshape(heads, HEAD_DIM, BLOCK)
            far_scores.append(jnp.sum(prod, axis=1))
            far_values.append(kv[width:])
        top = jnp.maximum(jnp.max(near, axis=1), jnp.max(hub, axis=1))
        for scored in far_scores:
            top = jnp.maximum(top, scored)
        near_exp = jnp.exp(near - top[:, None, :])
        hub_exp = jnp.exp(hub - top[:, None, :])
        total = jnp.sum(near_exp, axis=1) + jnp.sum(hub_exp, axis=1)
        mixed = dot_nn(
            by_head_cols(v_t[:, here]), near_exp.astype(BF16).reshape(heads * BLOCK, BLOCK)
        )
        mixed = mixed + dot_nn(vv_heads, hub_exp.astype(BF16).reshape(heads * n_virt, BLOCK))
        for scored, values in zip(far_scores, far_values):
            weight = jnp.exp(scored - top)
            total = total + weight
            mixed = mixed + expand(weight) * values
        attended = (mixed * expand(1.0 / total)).astype(BF16)
        residual = dot_nt(eye, feat) + dot_nn(wo_t, attended)
        hidden = layer_norm_cols(residual, gain_cols[0]).astype(BF16)
        inner = jax.nn.gelu(dot_nn(w1_t, hidden), approximate=True).astype(BF16)
        summed = hidden.astype(F32) + dot_nn(w2_t, inner)
        out[here, :] = jnp.transpose(layer_norm_cols(summed, gain_cols[1])).astype(BF16)
        return carry

    lax.fori_loop(0, nodes // BLOCK, step, 0)


def per_device(
    features,
    qkv_weight,
    out_weight,
    ffn_in,
    ffn_out,
    norm_gains,
    virtual_table,
    block_mask,
    halo_send,
    halo_links,
    expander_perm,
    virtual_ids,
):
    nodes, width = features.shape
    n_dom = lax.axis_size("dom")
    n_head = lax.axis_size("head")
    part = nodes // n_head
    halo = halo_send.shape[2]
    wqkv = jnp.transpose(qkv_weight, (1, 2, 0)).reshape(-1, width)
    w1 = ffn_in.T
    w_rows = wqkv.shape[0] + 2 * w1.shape[0]
    send = halo_send.reshape(2, halo)
    links = halo_links.T
    vids = virtual_ids.reshape(1, nodes)
    chunk = 512
    any_space = pl.BlockSpec(memory_space=pl.ANY)
    vmem = pl.BlockSpec(memory_space=pltpu.VMEM)
    smem = pl.BlockSpec(memory_space=pltpu.SMEM)
    dma = pltpu.SemaphoreType.DMA
    lists = halo // chunk
    pieces = part // chunk
    peer_feats, near_list, rows_a, rows_b, lookup, weights = pl.pallas_call(
        functools.partial(exchange_kernel, n_dom, n_head),
        name="exchange",
        out_shape=(
            jax.ShapeDtypeStruct((nodes, width), BF16),
            jax.ShapeDtypeStruct((halo, width), BF16),
            jax.ShapeDtypeStruct((part, width), BF16),
            jax.ShapeDtypeStruct((part, width), BF16),
            jax.ShapeDtypeStruct((2, halo), jnp.int32),
            jax.ShapeDtypeStruct((n_head, w_rows, width), BF16),
        ),
        in_specs=[vmem, smem, vmem, any_space, vmem, vmem, vmem],
        out_specs=(any_space, any_space, any_space, any_space, vmem, any_space),
        scratch_shapes=[
            pltpu.VMEM((nodes, width), F32),
            pltpu.VMEM((chunk, width), F32),
            pltpu.VMEM((lists + 2 * pieces, chunk, width), BF16),
            pltpu.VMEM((w_rows, width), BF16),
            pltpu.VMEM((2, halo), jnp.int32),
            pltpu.VMEM((2, part), jnp.int32),
            pltpu.SMEM((2, part), jnp.int32),
            dma((2,)),
            dma((2,)),
            dma((2,)),
            dma((2,)),
            dma((lists,)),
            dma((lists,)),
            dma((2 * pieces,)),
            dma((2 * pieces,)),
            dma((n_head - 1,)),
            dma((n_head,)),
            dma((3,)),
        ],
        compiler_params=pltpu.CompilerParams(
            collective_id=0, has_side_effects=True, vmem_limit_bytes=48 << 20
        ),
    )(features, send, send, expander_perm, wqkv, w1, ffn_out)

    head = lax.axis_index("head").astype(jnp.int32).reshape(1)
    grid_spec = pltpu.PrefetchScalarGridSpec(
        num_scalar_prefetch=1,
        grid=(1,),
        in_specs=[
            pl.BlockSpec((links.shape[0], part), lambda i, h: (0, h[0]), memory_space=pltpu.SMEM),
            pl.BlockSpec((1, 1, part), lambda i, h: (0, 0, h[0]), memory_space=pltpu.SMEM),
            smem,
            vmem,
            vmem,
            vmem,
            vmem,
            pl.BlockSpec((part, width), lambda i, h: (h[0], 0)),
            pl.BlockSpec((part, BLOCK), lambda i, h: (h[0], 0)),
            pl.BlockSpec((1, part), lambda i, h: (0, h[0])),
            vmem,
            vmem,
            vmem,
            vmem,
        ],
        out_specs=pl.BlockSpec((part, width), lambda i, h: (0, 0)),
        scratch_shapes=[
            pltpu.VMEM((nodes + halo, width), F32),
            pltpu.VMEM(((links.shape[0] + 1) * part, width), F32),
            pltpu.VMEM((width, part), F32),
            pltpu.VMEM((part, width), BF16),
            pltpu.VMEM((part, width), BF16),
            pltpu.VMEM((width, part), BF16),
            pltpu.VMEM((2 * width, width), BF16),
        ],
    )
    return pl.pallas_call(
        layer_kernel,
        name="layer",
        grid_spec=grid_spec,
        out_shape=jax.ShapeDtypeStruct((part, width), BF16),
        compiler_params=pltpu.CompilerParams(vmem_limit_bytes=48 << 20),
    )(
        head,
        links,
        expander_perm,
        lookup.reshape(2 * halo),
        peer_feats,
        near_list,
        rows_a,
        rows_b,
        features,
        block_mask,
        vids,
        virtual_table,
        weights,
        out_weight,
        norm_gains,
    )


def solution(mesh):
    return jax.shard_map(
        per_device,
        mesh=mesh,
        in_specs=(
            P("dom", None),
            P(None, None, "head"),
            P(),
            P(None, "head"),
            P("head", None),
            P(),
            P(),
            P("dom", None),
            P("dom", None, None),
            P("dom", None),
            P(None, "dom", None),
            P("dom"),
        ),
        out_specs=P(("dom", "head"), None),
        check_vma=False,
    )
```

```python
import functools

import jax
import jax.numpy as jnp
from jax import lax
from jax.experimental import pallas as pl
from jax.experimental.pallas import tpu as pltpu
from jax.sharding import PartitionSpec as P

HEAD_DIM = 16
BLOCK = 128
ROWS = 64
CHUNK = 512
MESH = pl.DeviceIdType.MESH
F32 = jnp.float32
BF16 = jnp.bfloat16
NEG = -1e30


def dot_nt(a, b):
    return lax.dot_general(a, b, (((1,), (1,)), ((), ())), preferred_element_type=F32)


def dot_nn(a, b):
    return jnp.dot(a, b, preferred_element_type=F32)


def iota(shape, dim):
    return lax.broadcasted_iota(jnp.int32, shape, dim)


def gather_rows(count, index, index_base, table, out, out_base):
    def step(i, carry):
        base = pl.multiple_of(i * ROWS, ROWS)
        for u in range(ROWS):
            row = index[index_base + base + u]
            out[pl.ds(out_base + base + u, 1), :] = table[pl.ds(row, 1), :]
        return carry

    lax.fori_loop(0, count // ROWS, step, 0)


def widen(source, source_base, out, out_base, rows):
    def step(i, carry):
        at = pl.multiple_of(i * 256, 256)
        out[pl.ds(out_base + at, 256), :] = source[pl.ds(source_base + at, 256), :].astype(F32)
        return carry

    lax.fori_loop(0, rows // 256, step, 0)


def layer_norm_cols(values, gain):
    count = values.shape[0]
    center = jnp.sum(values, axis=0, keepdims=True) * (1.0 / count)
    shifted = values - center
    second = jnp.sum(shifted * shifted, axis=0, keepdims=True) * (1.0 / count)
    return shifted * lax.rsqrt(second + 1e-05) * gain


def prepare(weights, wo, gains, vtab, own, wq_p, wkv_p, w1_t, w2_t, wo_t, gain_cols, q_rows, k_rows, q_t, v_t, vk_h, vv_h):
    n_head, _, width = weights.shape
    local = width // n_head
    heads = width // HEAD_DIM
    f_rows = (weights.shape[1] - 3 * local) // 2

    def whole(lo, count):
        return jnp.concatenate([weights[h, lo : lo + count, :] for h in range(n_head)], axis=0)

    row, col = iota((width, width), 0), iota((width, width), 1)
    order = (col == lax.rem(row, heads) * HEAD_DIM + row // heads).astype(BF16)
    eye = (row == col).astype(BF16)
    scale = HEAD_DIM ** (-0.5)
    wq = (dot_nn(order, whole(0, local)) * scale).astype(BF16)
    wk = dot_nn(order, whole(local, local)).astype(BF16)
    wv = dot_nn(order, whole(2 * local, local)).astype(BF16)
    wkv_p[0:width, :] = wk
    wkv_p[width : 2 * width, :] = wv
    w1_t[...] = whole(3 * local, f_rows)
    w2_t[...] = dot_nt(eye, whole(3 * local + f_rows, f_rows)).astype(BF16)
    wo_t[...] = dot_nt(eye, dot_nn(order, wo[...]).astype(BF16)).astype(BF16)
    for g in (0, 1):
        gain_cols[g] = jnp.transpose(jnp.broadcast_to(gains[g : g + 1, :], (width, width)))
    q_rows[...] = dot_nt(own, wq).astype(BF16)
    k_rows[...] = dot_nt(own, wk).astype(BF16)
    q_t[...] = dot_nt(wq, own).astype(BF16).astype(F32)
    v_t[...] = dot_nt(wv, own).astype(BF16)
    vk = dot_nt(vtab, wk).astype(BF16)
    vv = dot_nt(wv, vtab).astype(BF16)
    zero = jnp.zeros((), BF16)
    vk_h[...] = jnp.concatenate(
        [jnp.where(lax.rem(iota(vk.shape, 1), heads) == h, vk, zero) for h in range(heads)], axis=0
    )
    vv_h[...] = jnp.concatenate(
        [jnp.where(lax.rem(iota(vv.shape, 0), heads) == h, vv, zero) for h in range(heads)], axis=1
    )


def near_block(b, mask, vids, q_rows, k_rows, v_t, vk_h, vv_h, near_out, near_top, near_sum, fill=None):
    width = q_rows.shape[1]
    heads = width // HEAD_DIM
    n_virt = vk_h.shape[0] // heads
    here = pl.ds(b * BLOCK, BLOCK) if isinstance(b, int) else pl.ds(pl.multiple_of(b * BLOCK, BLOCK), BLOCK)
    row, col = iota((BLOCK, BLOCK), 0), iota((BLOCK, BLOCK), 1)
    eye = (row == col).astype(BF16)
    bias = jnp.where((mask[here, :] > 0) | (row == col), 0.0, NEG).astype(BF16)
    bias_t = dot_nt(eye, bias)
    zero = jnp.zeros((), BF16)
    keys, queries, values = k_rows[here, :], q_rows[here, :], v_t[:, here]
    lane_h, sub_h = lax.rem(iota((BLOCK, width), 1), heads), lax.rem(iota((width, BLOCK), 0), heads)
    scores = dot_nt(
        jnp.concatenate([jnp.where(lane_h == h, keys, zero) for h in range(heads)], axis=0), queries
    )
    hub = dot_nt(vk_h[...], queries)
    mine = vids[0:1, here] == iota((n_virt, BLOCK), 0)
    tops, sums, near_p, hub_p = [], [], [], []
    for h in range(heads):
        near = scores[h * BLOCK : (h + 1) * BLOCK] + bias_t
        virt = jnp.where(mine, hub[h * n_virt : (h + 1) * n_virt], NEG)
        top = jnp.maximum(
            jnp.max(near, axis=0, keepdims=True), jnp.max(virt, axis=0, keepdims=True)
        )
        near = jnp.exp(near - top)
        virt = jnp.exp(virt - top)
        tops.append(top)
        sums.append(jnp.sum(near, axis=0, keepdims=True) + jnp.sum(virt, axis=0, keepdims=True))
        near_p.append(near.astype(BF16))
        hub_p.append(virt)
        if fill is not None:
            fill(h)
    near_top[:, here] = jnp.concatenate(tops, axis=0)
    near_sum[:, here] = jnp.concatenate(sums, axis=0)
    by_head = jnp.concatenate([jnp.where(sub_h == h, values, zero) for h in range(heads)], axis=1)
    near_out[:, here] = dot_nn(by_head, jnp.concatenate(near_p, axis=0)) + dot_nn(
        vv_h[...], jnp.concatenate(hub_p, axis=0).astype(BF16)
    )


def far_chunk(c, size, row_refs, wkv_p, q_t, near_out, near_top, near_sum, attended):
    width = q_t.shape[0]
    heads = width // HEAD_DIM
    at = c * size if isinstance(c, int) else pl.multiple_of(c * size, size)
    here = pl.ds(at, size)
    split = (HEAD_DIM, heads, size)
    queries = q_t[:, here].reshape(split)
    wkv = wkv_p[...]
    scored, values = [], []
    for ref, first in row_refs:
        rows = ref[pl.ds(first + at, size), :].astype(BF16)
        kv = dot_nt(wkv, rows)
        keys = kv[0:width].astype(BF16).astype(F32).reshape(split)
        scored.append(jnp.sum(keys * queries, axis=0))
        values.append(kv[width:].reshape(split))
    top = near_top[:, here]
    for s in scored:
        top = jnp.maximum(top, s)
    shrink = jnp.exp(near_top[:, here] - top)
    total = near_sum[:, here] * shrink
    mixed = near_out[:, here].reshape(split) * shrink[None]
    for s, v in zip(scored, values):
        weight = jnp.exp(s - top)
        total = total + weight
        mixed = mixed + v * weight[None]
    attended[:, here] = (mixed * (1.0 / total)[None]).reshape(width, size).astype(BF16)


def ffn_chunk(c, size, own, attended, wo_t, w1_t, w2_t, gain_cols, out):
    width = attended.shape[0]
    at = c * size if isinstance(c, int) else pl.multiple_of(c * size, size)
    here = pl.ds(at, size)
    eye = (iota((width, width), 0) == iota((width, width), 1)).astype(BF16)
    gain = [jnp.concatenate([gain_cols[g]] * (size // width), axis=1) for g in (0, 1)]
    residual = dot_nt(eye, own(here)) + dot_nn(wo_t[...], attended[:, here])
    hidden = layer_norm_cols(residual, gain[0]).astype(BF16)
    inner = jax.nn.gelu(dot_nn(w1_t[...], hidden), approximate=True).astype(BF16)
    summed = layer_norm_cols(hidden.astype(F32) + dot_nn(w2_t[...], inner), gain[1])
    for k in range(size // width):
        out[pl.ds(at + k * width, width), :] = jnp.transpose(
            summed[:, k * width : (k + 1) * width]
        ).astype(BF16)


def layer_kernel(
    n_dom,
    n_head,
    feats_in,
    wqkv_in,
    wo_in,
    w1_in,
    w2_in,
    gains_in,
    vtab_in,
    mask_in,
    send_in,
    links_in,
    perm_in,
    vids_in,
    out,
    feats,
    table,
    staged,
    packed,
    weights,
    wo,
    gains,
    vtab,
    mask,
    vids,
    send_first,
    send_second,
    links,
    request,
    wanted,
    lists,
    matched,
    far,
    wq_p,
    wkv_p,
    w1_t,
    w2_t,
    wo_t,
    gain_cols,
    q_rows,
    k_rows,
    q_t,
    v_t,
    vk_h,
    vv_h,
    near_out,
    near_top,
    near_sum,
    attended,
    local_sems,
    req_send,
    req_recv,
    list_send,
    list_recv,
    rows_send,
    rows_recv,
    w_send,
    w_recv,
):
    nodes = feats.shape[0]
    part = out.shape[0]
    halo = lists.shape[0] // 2
    chunk = staged.shape[0]
    link_count = links_in.shape[0]
    dom = lax.axis_index("dom")
    head = lax.axis_index("head")
    core = lax.rem(dom, 2)
    peer = dom + 1 - 2 * core
    side = lax.rem(dom + 2 * core - 1 + n_dom, n_dom)
    levels = n_dom.bit_length() - 1
    mine = pl.ds(pl.multiple_of(head * part, part), part)

    def flipped(stride):
        bit = lax.rem(dom // (1 << stride), 2)
        return dom + (1 - 2 * bit) * (1 << stride)

    partners = [flipped(m * (levels - 1) // 2) for m in range(3)]
    others = [lax.rem(head + k, n_head) for k in range(1, n_head)]

    barrier = pltpu.get_barrier_semaphore()
    for dev in [side] + partners:
        pl.semaphore_signal(barrier, inc=1, device_id={"dom": dev}, device_id_type=MESH)
    for dev in others:
        pl.semaphore_signal(barrier, inc=1, device_id={"head": dev}, device_id_type=MESH)

    def fetch(k, src, dst):
        copy = pltpu.make_async_copy(src, dst, local_sems.at[k])
        copy.start()
        return copy

    q_rows_in, f_rows = wqkv_in.shape[0], w1_in.shape[0]
    got_feats = fetch(0, feats_in, feats)
    got_first = fetch(1, send_in.at[0, core], send_first)
    got_second = fetch(2, send_in.at[0, 1 - core], send_second)
    got_weights = [
        fetch(3, wqkv_in, weights.at[head, pl.ds(0, q_rows_in)]),
        fetch(4, w1_in, weights.at[head, pl.ds(q_rows_in, f_rows)]),
        fetch(5, w2_in, weights.at[head, pl.ds(q_rows_in + f_rows, f_rows)]),
    ]
    got_rest = [
        fetch(6, wo_in, wo),
        fetch(7, gains_in, gains),
        fetch(8, vtab_in, vtab),
        fetch(9, mask_in.at[mine], mask),
        fetch(10, vids_in.at[:, mine], vids),
    ]
    got_links = [
        fetch(11 + e, links_in.at[e, mine], links.at[pl.ds(e * part, part)]) for e in range(link_count)
    ]

    def remote(src, dst, send, recv, device):
        return pltpu.make_async_remote_copy(
            src_ref=src, dst_ref=dst, send_sem=send, recv_sem=recv, device_id=device, device_id_type=MESH
        )

    pl.semaphore_wait(barrier, 4 + len(others))
    requests = []
    for m in range(3):
        copy = remote(
            perm_in.at[m, 0, mine], request.at[pl.ds(m * part, part)], req_send.at[m], req_recv.at[m], {"dom": partners[m]}
        )
        copy.start()
        requests.append(copy)
    for copy in got_weights:
        copy.wait()
    w_copies = []
    for k, dev in enumerate(others):
        copy = remote(weights.at[head], weights.at[head], w_send.at[k], w_recv.at[head], {"head": dev})
        copy.start()
        w_copies.append(copy)

    got_feats.wait()
    widen(feats, 0, table, 0, nodes)

    sent = []

    def send_chunk(index, at, dst, send, recv, device):
        slot = len(sent)
        gather_rows(chunk, index, at, table, staged, 0)
        packed[slot] = staged[...].astype(BF16)
        copy = remote(packed.at[slot], dst, send, recv, device)
        copy.start()
        sent.append(copy)

    count = halo // chunk
    for k, (got, index, row, dev) in enumerate(
        ((got_first, send_first, core, side), (got_second, send_second, 1 - core, peer))
    ):
        got.wait()
        for i in range(count):
            at = pl.multiple_of((1 - row) * halo + i * chunk, chunk)
            s = k * count + i
            send_chunk(
                index, i * chunk, lists.at[pl.ds(at, chunk)], list_send.at[s], list_recv.at[s], {"dom": dev}
            )
    list_copies = list(sent)

    for copy in requests:
        copy.wait_recv()
    got_wanted = [
        fetch(11 + link_count + m, request.at[pl.ds(m * part, part)], wanted.at[pl.ds(m * part, part)]) for m in range(3)
    ]
    pieces = part // chunk
    for m in (1, 2, 0):
        got_wanted[m].wait()
        for i in range(pieces):
            s = m * pieces + i
            send_chunk(
                wanted,
                m * part + i * chunk,
                matched.at[m, pl.ds(i * chunk, chunk)],
                rows_send.at[s],
                rows_recv.at[s],
                {"dom": partners[m]},
            )

    for dev in others:
        remote(weights.at[head], weights.at[dev], w_send.at[0], w_recv.at[dev], {"head": dev}).wait_recv()
    for copy in got_rest:
        copy.wait()
    prepare(
        weights, wo, gains, vtab[...], feats[mine, :], wq_p, wkv_p, w1_t, w2_t, wo_t, gain_cols,
        q_rows, k_rows, q_t, v_t, vk_h, vv_h,
    )
    for b in range(part // BLOCK):
        near_block(b, mask, vids, q_rows, k_rows, v_t, vk_h, vv_h, near_out, near_top, near_sum)

    for copy in list_copies:
        copy.wait_recv()
    widen(lists, 0, table, 0, 2 * halo)
    for copy in got_links:
        copy.wait()
    gather_rows(link_count * part, links, 0, table, far, 0)

    for copy in sent[len(list_copies) :]:
        copy.wait_recv()
    row_refs = [(far, e * part) for e in range(link_count)] + [(matched.at[m], 0) for m in range(3)]
    for c in range(part // 256):
        far_chunk(c, 256, row_refs, wkv_p, q_t, near_out, near_top, near_sum, attended)
    own_base = pl.multiple_of(head * part, part)
    ffn_chunk(
        0,
        part,
        lambda here: feats[pl.ds(own_base + here.start, here.size), :],
        attended,
        wo_t,
        w1_t,
        w2_t,
        gain_cols,
        out,
    )
    for copy in requests + w_copies + sent:
        copy.wait_send()


def per_device(
    features,
    qkv_weight,
    out_weight,
    ffn_in,
    ffn_out,
    norm_gains,
    virtual_table,
    block_mask,
    halo_send,
    halo_links,
    expander_perm,
    virtual_ids,
):
    nodes, width = features.shape
    n_dom = lax.axis_size("dom")
    n_head = lax.axis_size("head")
    part = nodes // n_head
    halo = halo_send.shape[2]
    heads = width // HEAD_DIM
    n_virt = virtual_table.shape[0]
    wqkv = jnp.transpose(qkv_weight, (1, 2, 0)).reshape(-1, width)
    w1 = ffn_in.T
    w_rows = wqkv.shape[0] + 2 * w1.shape[0]
    hidden = n_head * w1.shape[0]
    links = halo_links.T
    link_count = links.shape[0]
    vids = virtual_ids.reshape(1, nodes)
    chunk = CHUNK
    lists = 2 * halo // chunk
    pieces = 3 * part // chunk
    i32 = jnp.int32
    dma = pltpu.SemaphoreType.DMA
    return pl.pallas_call(
        functools.partial(layer_kernel, n_dom, n_head),
        name="layer",
        out_shape=jax.ShapeDtypeStruct((part, width), BF16),
        in_specs=[pl.BlockSpec(memory_space=pl.ANY)] * 12,
        out_specs=pl.BlockSpec(memory_space=pltpu.VMEM),
        scratch_shapes=[
            pltpu.VMEM((nodes, width), BF16),
            pltpu.VMEM((nodes, width), F32),
            pltpu.VMEM((chunk, width), F32),
            pltpu.VMEM((lists + pieces, chunk, width), BF16),
            pltpu.VMEM((n_head, w_rows, width), BF16),
            pltpu.VMEM((width, width), BF16),
            pltpu.VMEM((2, width), F32),
            pltpu.VMEM((n_virt, width), BF16),
            pltpu.VMEM((part, BLOCK), i32),
            pltpu.VMEM((1, part), i32),
            pltpu.SMEM((halo,), i32),
            pltpu.SMEM((halo,), i32),
            pltpu.SMEM((link_count * part,), i32),
            pltpu.VMEM((3 * part,), i32),
            pltpu.SMEM((3 * part,), i32),
            pltpu.VMEM((2 * halo, width), BF16),
            pltpu.VMEM((3, part, width), BF16),
            pltpu.VMEM((link_count * part, width), F32),
            pltpu.VMEM((width, width), BF16),
            pltpu.VMEM((2 * width, width), BF16),
            pltpu.VMEM((hidden, width), BF16),
            pltpu.VMEM((width, hidden), BF16),
            pltpu.VMEM((width, width), BF16),
            pltpu.VMEM((2, width, width), F32),
            pltpu.VMEM((part, width), BF16),
            pltpu.VMEM((part, width), BF16),
            pltpu.VMEM((width, part), F32),
            pltpu.VMEM((width, part), BF16),
            pltpu.VMEM((heads * n_virt, width), BF16),
            pltpu.VMEM((width, heads * n_virt), BF16),
            pltpu.VMEM((width, part), F32),
            pltpu.VMEM((heads, part), F32),
            pltpu.VMEM((heads, part), F32),
            pltpu.VMEM((width, part), BF16),
            dma((14 + link_count,)),
            dma((3,)),
            dma((3,)),
            dma((lists,)),
            dma((lists,)),
            dma((pieces,)),
            dma((pieces,)),
            dma((n_head - 1,)),
            dma((n_head,)),
        ],
        compiler_params=pltpu.CompilerParams(
            collective_id=0, has_side_effects=True, vmem_limit_bytes=60 << 20
        ),
    )(
        features,
        wqkv,
        out_weight,
        w1,
        ffn_out,
        norm_gains,
        virtual_table,
        block_mask,
        halo_send,
        links,
        expander_perm,
        vids,
    )


def solution(mesh):
    return jax.shard_map(
        per_device,
        mesh=mesh,
        in_specs=(
            P("dom", None),
            P(None, None, "head"),
            P(),
            P(None, "head"),
            P("head", None),
            P(),
            P(),
            P("dom", None),
            P("dom", None, None),
            P("dom", None),
            P(None, "dom", None),
            P("dom"),
        ),
        out_specs=P(("dom", "head"), None),
        check_vma=False,
    )
```

```python
import functools

import jax
import jax.numpy as jnp
from jax import lax
from jax.experimental import pallas as pl
from jax.experimental.pallas import tpu as pltpu
from jax.sharding import PartitionSpec as P

HEAD_DIM = 16
BLOCK = 128
CHUNK = 512
MESH = pl.DeviceIdType.MESH
F32 = jnp.float32
BF16 = jnp.bfloat16
NEG = -1e30


def dot_nt(a, b):
    return lax.dot_general(a, b, (((1,), (1,)), ((), ())), preferred_element_type=F32)


def dot_nn(a, b):
    return jnp.dot(a, b, preferred_element_type=F32)


def iota(shape, dim):
    return lax.broadcasted_iota(jnp.int32, shape, dim)


def gather_rows(count, index, first, table, out, out_first):
    for u in range(count):
        out[out_first + u : out_first + u + 1, :] = table[pl.ds(index[first + u], 1), :]


def widen(source, source_base, out, out_base, rows):
    def step(i, carry):
        at = pl.multiple_of(i * 256, 256)
        out[pl.ds(out_base + at, 256), :] = source[pl.ds(source_base + at, 256), :].astype(F32)
        return carry

    lax.fori_loop(0, rows // 256, step, 0)


def layer_norm_cols(values, gain):
    count = values.shape[0]
    center = jnp.sum(values, axis=0, keepdims=True) * (1.0 / count)
    shifted = values - center
    second = jnp.sum(shifted * shifted, axis=0, keepdims=True) * (1.0 / count)
    return shifted * lax.rsqrt(second + 1e-05) * gain


def prepare(weights, wo, gains, vtab, own, wq_p, wkv_p, w1_t, w2_t, wo_t, gain_cols, q_rows, k_rows, q_t, v_t, vk_h, vv_h):
    n_head, _, width = weights.shape
    local = width // n_head
    heads = width // HEAD_DIM
    f_rows = (weights.shape[1] - 3 * local) // 2

    def whole(lo, count):
        return jnp.concatenate([weights[h, lo : lo + count, :] for h in range(n_head)], axis=0)

    row, col = iota((width, width), 0), iota((width, width), 1)
    order = (col == lax.rem(row, heads) * HEAD_DIM + row // heads).astype(BF16)
    eye = (row == col).astype(BF16)
    scale = HEAD_DIM ** (-0.5)
    wq = (dot_nn(order, whole(0, local)) * scale).astype(BF16)
    wk = dot_nn(order, whole(local, local)).astype(BF16)
    wv = dot_nn(order, whole(2 * local, local)).astype(BF16)
    wkv_p[0:width, :] = wk
    wkv_p[width : 2 * width, :] = wv
    w1_t[...] = whole(3 * local, f_rows)
    w2_t[...] = dot_nt(eye, whole(3 * local + f_rows, f_rows)).astype(BF16)
    wo_t[...] = dot_nt(eye, dot_nn(order, wo[...]).astype(BF16)).astype(BF16)
    for g in (0, 1):
        gain_cols[g] = jnp.transpose(jnp.broadcast_to(gains[g : g + 1, :], (width, width)))
    q_rows[...] = dot_nt(own, wq).astype(BF16)
    k_rows[...] = dot_nt(own, wk).astype(BF16)
    q_t[...] = dot_nt(wq, own).astype(BF16).astype(F32)
    v_t[...] = dot_nt(wv, own).astype(BF16)
    vk = dot_nt(vtab, wk).astype(BF16)
    vv = dot_nt(wv, vtab).astype(BF16)
    zero = jnp.zeros((), BF16)
    vk_h[...] = jnp.concatenate(
        [jnp.where(lax.rem(iota(vk.shape, 1), heads) == h, vk, zero) for h in range(heads)], axis=0
    )
    vv_h[...] = jnp.concatenate(
        [jnp.where(lax.rem(iota(vv.shape, 0), heads) == h, vv, zero) for h in range(heads)], axis=1
    )


def near_block(b, mask, vids, q_rows, k_rows, v_t, vk_h, vv_h, near_out, near_top, near_sum):
    width = q_rows.shape[1]
    heads = width // HEAD_DIM
    n_virt = vk_h.shape[0] // heads
    here = pl.ds(b * BLOCK, BLOCK) if isinstance(b, int) else pl.ds(pl.multiple_of(b * BLOCK, BLOCK), BLOCK)
    row, col = iota((BLOCK, BLOCK), 0), iota((BLOCK, BLOCK), 1)
    eye = (row == col).astype(BF16)
    bias = jnp.where((mask[here, :] > 0) | (row == col), 0.0, NEG).astype(BF16)
    bias_t = dot_nt(eye, bias)
    zero = jnp.zeros((), BF16)
    keys, queries, values = k_rows[here, :], q_rows[here, :], v_t[:, here]
    lane_h, sub_h = lax.rem(iota((BLOCK, width), 1), heads), lax.rem(iota((width, BLOCK), 0), heads)
    scores = dot_nt(
        keys, jnp.concatenate([jnp.where(lane_h == h, queries, zero) for h in range(heads)], axis=0)
    )
    hub = dot_nt(vk_h[...], queries)
    mine = vids[0:1, here] == iota((n_virt, BLOCK), 0)
    tops, sums, near_p, hub_p = [], [], [], []
    for h in range(heads):
        near = scores[:, h * BLOCK : (h + 1) * BLOCK] + bias_t
        virt = jnp.where(mine, hub[h * n_virt : (h + 1) * n_virt], NEG)
        top = jnp.maximum(
            jnp.max(near, axis=0, keepdims=True), jnp.max(virt, axis=0, keepdims=True)
        )
        near = jnp.exp(near - top)
        virt = jnp.exp(virt - top)
        tops.append(top)
        sums.append(jnp.sum(near, axis=0, keepdims=True) + jnp.sum(virt, axis=0, keepdims=True))
        near_p.append(near.astype(BF16))
        hub_p.append(virt)
    near_top[:, here] = jnp.concatenate(tops, axis=0)
    near_sum[:, here] = jnp.concatenate(sums, axis=0)
    by_head = jnp.concatenate([jnp.where(sub_h == h, values, zero) for h in range(heads)], axis=1)
    near_out[:, here] = dot_nn(by_head, jnp.concatenate(near_p, axis=0)) + dot_nn(
        vv_h[...], jnp.concatenate(hub_p, axis=0).astype(BF16)
    )


def far_chunk(c, size, row_refs, wkv_p, q_t, near_out, near_top, near_sum, attended):
    width = q_t.shape[0]
    heads = width // HEAD_DIM
    at = c * size if isinstance(c, int) else pl.multiple_of(c * size, size)
    here = pl.ds(at, size)
    split = (HEAD_DIM, heads, size)
    queries = q_t[:, here].reshape(split)
    wkv = wkv_p[...]
    scored, values = [], []
    for ref, first in row_refs:
        rows = ref[pl.ds(first + at, size), :].astype(BF16)
        kv = dot_nt(wkv, rows)
        keys = kv[0:width].astype(BF16).astype(F32).reshape(split)
        scored.append(jnp.sum(keys * queries, axis=0))
        values.append(kv[width:].reshape(split))
    top = near_top[:, here]
    for s in scored:
        top = jnp.maximum(top, s)
    shrink = jnp.exp(near_top[:, here] - top)
    total = near_sum[:, here] * shrink
    mixed = near_out[:, here].reshape(split) * shrink[None]
    for s, v in zip(scored, values):
        weight = jnp.exp(s - top)
        total = total + weight
        mixed = mixed + v * weight[None]
    attended[:, here] = (mixed * (1.0 / total)[None]).reshape(width, size).astype(BF16)


def ffn_chunk(c, size, own, attended, wo_t, w1_t, w2_t, gain_cols, out):
    width = attended.shape[0]
    at = c * size if isinstance(c, int) else pl.multiple_of(c * size, size)
    here = pl.ds(at, size)
    eye = (iota((width, width), 0) == iota((width, width), 1)).astype(BF16)
    gain = [jnp.concatenate([gain_cols[g]] * (size // width), axis=1) for g in (0, 1)]
    residual = dot_nt(eye, own(here)) + dot_nn(wo_t[...], attended[:, here])
    hidden = layer_norm_cols(residual, gain[0]).astype(BF16)
    inner = jax.nn.gelu(dot_nn(w1_t[...], hidden), approximate=True).astype(BF16)
    summed = layer_norm_cols(hidden.astype(F32) + dot_nn(w2_t[...], inner), gain[1])
    for k in range(size // width):
        out[pl.ds(at + k * width, width), :] = jnp.transpose(
            summed[:, k * width : (k + 1) * width]
        ).astype(BF16)


def layer_kernel(
    n_dom,
    n_head,
    feats_in,
    wqkv_in,
    wo_in,
    w1_in,
    w2_in,
    gains_in,
    vtab_in,
    mask_in,
    send_in,
    links_in,
    perm_in,
    vids_in,
    out,
    feats,
    table,
    staged,
    packed,
    weights,
    wo,
    gains,
    vtab,
    mask,
    vids,
    send_first,
    send_second,
    links,
    wanted,
    lists,
    matched,
    far,
    wq_p,
    wkv_p,
    w1_t,
    w2_t,
    wo_t,
    gain_cols,
    q_rows,
    k_rows,
    q_t,
    v_t,
    vk_h,
    vv_h,
    near_out,
    near_top,
    near_sum,
    attended,
    local_sems,
    req_send,
    req_recv,
    list_send,
    list_recv,
    rows_send,
    rows_recv,
    w_send,
    w_recv,
    pass_send,
    pass_recv,
):
    nodes = feats.shape[0]
    part = out.shape[0]
    halo = lists.shape[0] // 2
    chunk = staged.shape[0]
    link_count = links_in.shape[0]
    dom = lax.axis_index("dom")
    head = lax.axis_index("head")
    core = lax.rem(dom, 2)
    peer = dom + 1 - 2 * core
    side = lax.rem(dom + 2 * core - 1 + n_dom, n_dom)
    levels = n_dom.bit_length() - 1
    mine = pl.ds(pl.multiple_of(head * part, part), part)

    def flipped(stride):
        bit = lax.rem(dom // (1 << stride), 2)
        return dom + (1 - 2 * bit) * (1 << stride)

    partners = [flipped(m * (levels - 1) // 2) for m in range(3)]
    others = [lax.rem(head + k, n_head) for k in range(1, n_head)]

    barrier = pltpu.get_barrier_semaphore()
    for dev in [side] + partners:
        pl.semaphore_signal(barrier, inc=1, device_id={"dom": dev}, device_id_type=MESH)
    for dev in others:
        pl.semaphore_signal(barrier, inc=1, device_id={"head": dev}, device_id_type=MESH)

    def fetch(k, src, dst):
        copy = pltpu.make_async_copy(src, dst, local_sems.at[k])
        copy.start()
        return copy

    q_rows_in, f_rows = wqkv_in.shape[0], w1_in.shape[0]
    got_feats = fetch(0, feats_in, feats)
    share = send_first.shape[0]
    got_first = fetch(1, send_in.at[0, core, pl.ds(pl.multiple_of(head * share, share), share)], send_first)
    got_second = fetch(2, send_in.at[0, 1 - core], send_second)
    got_weights = [
        fetch(3, wqkv_in, weights.at[head, pl.ds(0, q_rows_in)]),
        fetch(4, w1_in, weights.at[head, pl.ds(q_rows_in, f_rows)]),
        fetch(5, w2_in, weights.at[head, pl.ds(q_rows_in + f_rows, f_rows)]),
    ]
    got_rest = [
        fetch(6, wo_in, wo),
        fetch(7, gains_in, gains),
        fetch(8, vtab_in, vtab),
        fetch(9, mask_in.at[mine], mask),
        fetch(10, vids_in.at[:, mine], vids),
    ]
    got_links = [
        fetch(11 + e, links_in.at[e, mine], links.at[pl.ds(e * part, part)]) for e in range(link_count)
    ]

    def remote(src, dst, send, recv, device):
        return pltpu.make_async_remote_copy(
            src_ref=src, dst_ref=dst, send_sem=send, recv_sem=recv, device_id=device, device_id_type=MESH
        )

    pl.semaphore_wait(barrier, 4 + len(others))
    requests = []
    for m in range(3):
        copy = remote(
            perm_in.at[m, 0, mine], wanted.at[pl.ds(m * part, part)], req_send.at[m], req_recv.at[m], {"dom": partners[m]}
        )
        copy.start()
        requests.append(copy)
    for copy in got_weights:
        copy.wait()
    w_copies = []
    for k, dev in enumerate(others):
        copy = remote(weights.at[head], weights.at[head], w_send.at[k], w_recv.at[head], {"head": dev})
        copy.start()
        w_copies.append(copy)

    got_feats.wait()
    widen(feats, 0, table, 0, nodes)

    sent = []

    def send_chunk(index, at, dst, send, recv, device):
        slot = len(sent)
        gather_rows(chunk, index, at, table, staged, 0)
        packed[slot] = staged[...].astype(BF16)
        copy = remote(packed.at[slot], dst, send, recv, device)
        copy.start()
        sent.append(copy)

    def shared(base, h):
        return lists.at[pl.ds(pl.multiple_of(base * halo + h * share, share), share)]

    got_first.wait()
    send_chunk(send_first, 0, shared(1 - core, head), list_send.at[0], list_recv.at[0], {"dom": side})
    got_second.wait()
    count = halo // chunk
    for i in range(count):
        at = pl.multiple_of(core * halo + i * chunk, chunk)
        send_chunk(
            send_second,
            i * chunk,
            lists.at[pl.ds(at, chunk)],
            list_send.at[1 + i],
            list_recv.at[1 + i],
            {"dom": peer},
        )
    list_copies = list(sent)

    pieces = part // chunk
    passed = []
    for m in (1, 2, 0):
        if m == 0:
            list_copies[0].wait_recv()
            for k, dev in enumerate(others):
                copy = remote(
                    shared(core, head), shared(core, head), pass_send.at[k], pass_recv.at[head], {"head": dev}
                )
                copy.start()
                passed.append(copy)
        requests[m].wait_recv()
        for i in range(pieces):
            s = m * pieces + i
            send_chunk(
                wanted,
                m * part + i * chunk,
                matched.at[m, pl.ds(i * chunk, chunk)],
                rows_send.at[s],
                rows_recv.at[s],
                {"dom": partners[m]},
            )

    for dev in others:
        remote(weights.at[head], weights.at[dev], w_send.at[0], w_recv.at[dev], {"head": dev}).wait_recv()
    for copy in got_rest:
        copy.wait()
    prepare(
        weights, wo, gains, vtab[...], feats[mine, :], wq_p, wkv_p, w1_t, w2_t, wo_t, gain_cols,
        q_rows, k_rows, q_t, v_t, vk_h, vv_h,
    )
    for b in range(part // BLOCK):
        near_block(b, mask, vids, q_rows, k_rows, v_t, vk_h, vv_h, near_out, near_top, near_sum)

    for dev in others:
        remote(
            shared(core, head), shared(core, dev), pass_send.at[0], pass_recv.at[dev], {"head": dev}
        ).wait_recv()
    for copy in list_copies[1:]:
        copy.wait_recv()
    widen(lists, 0, table, 0, 2 * halo)
    for copy in got_links:
        copy.wait()
    gather_rows(link_count * part, links, 0, table, far, 0)

    for copy in sent[len(list_copies) :]:
        copy.wait_recv()
    row_refs = [(far, e * part) for e in range(link_count)] + [(matched.at[m], 0) for m in range(3)]
    for c in range(part // 256):
        far_chunk(c, 256, row_refs, wkv_p, q_t, near_out, near_top, near_sum, attended)
    own_base = pl.multiple_of(head * part, part)
    ffn_chunk(
        0,
        part,
        lambda here: feats[pl.ds(own_base + here.start, here.size), :],
        attended,
        wo_t,
        w1_t,
        w2_t,
        gain_cols,
        out,
    )
    for copy in requests + w_copies + sent + passed:
        copy.wait_send()


def per_device(
    features,
    qkv_weight,
    out_weight,
    ffn_in,
    ffn_out,
    norm_gains,
    virtual_table,
    block_mask,
    halo_send,
    halo_links,
    expander_perm,
    virtual_ids,
):
    nodes, width = features.shape
    n_dom = lax.axis_size("dom")
    n_head = lax.axis_size("head")
    part = nodes // n_head
    halo = halo_send.shape[2]
    heads = width // HEAD_DIM
    n_virt = virtual_table.shape[0]
    wqkv = jnp.transpose(qkv_weight, (1, 2, 0)).reshape(-1, width)
    w1 = ffn_in.T
    w_rows = wqkv.shape[0] + 2 * w1.shape[0]
    hidden = n_head * w1.shape[0]
    links = halo_links.T
    link_count = links.shape[0]
    vids = virtual_ids.reshape(1, nodes)
    chunk = CHUNK
    share = halo // n_head
    lists = 1 + halo // chunk
    pieces = 3 * part // chunk
    i32 = jnp.int32
    dma = pltpu.SemaphoreType.DMA
    return pl.pallas_call(
        functools.partial(layer_kernel, n_dom, n_head),
        name="layer",
        out_shape=jax.ShapeDtypeStruct((part, width), BF16),
        in_specs=[pl.BlockSpec(memory_space=pl.ANY)] * 12,
        out_specs=pl.BlockSpec(memory_space=pltpu.VMEM),
        scratch_shapes=[
            pltpu.VMEM((nodes, width), BF16),
            pltpu.VMEM((nodes, width), F32),
            pltpu.VMEM((chunk, width), F32),
            pltpu.VMEM((lists + pieces, chunk, width), BF16),
            pltpu.VMEM((n_head, w_rows, width), BF16),
            pltpu.VMEM((width, width), BF16),
            pltpu.VMEM((2, width), F32),
            pltpu.VMEM((n_virt, width), BF16),
            pltpu.VMEM((part, BLOCK), i32),
            pltpu.VMEM((1, part), i32),
            pltpu.SMEM((share,), i32),
            pltpu.SMEM((halo,), i32),
            pltpu.SMEM((link_count * part,), i32),
            pltpu.SMEM((3 * part,), i32),
            pltpu.VMEM((2 * halo, width), BF16),
            pltpu.VMEM((3, part, width), BF16),
            pltpu.VMEM((link_count * part, width), F32),
            pltpu.VMEM((width, width), BF16),
            pltpu.VMEM((2 * width, width), BF16),
            pltpu.VMEM((hidden, width), BF16),
            pltpu.VMEM((width, hidden), BF16),
            pltpu.VMEM((width, width), BF16),
            pltpu.VMEM((2, width, width), F32),
            pltpu.VMEM((part, width), BF16),
            pltpu.VMEM((part, width), BF16),
            pltpu.VMEM((width, part), F32),
            pltpu.VMEM((width, part), BF16),
            pltpu.VMEM((heads * n_virt, width), BF16),
            pltpu.VMEM((width, heads * n_virt), BF16),
            pltpu.VMEM((width, part), F32),
            pltpu.VMEM((heads, part), F32),
            pltpu.VMEM((heads, part), F32),
            pltpu.VMEM((width, part), BF16),
            dma((11 + link_count,)),
            dma((3,)),
            dma((3,)),
            dma((lists,)),
            dma((lists,)),
            dma((pieces,)),
            dma((pieces,)),
            dma((n_head - 1,)),
            dma((n_head,)),
            dma((n_head - 1,)),
            dma((n_head,)),
        ],
        compiler_params=pltpu.CompilerParams(
            collective_id=0, has_side_effects=True, vmem_limit_bytes=60 << 20
        ),
    )(
        features,
        wqkv,
        out_weight,
        w1,
        ffn_out,
        norm_gains,
        virtual_table,
        block_mask,
        halo_send,
        links,
        expander_perm,
        vids,
    )


def solution(mesh):
    return jax.shard_map(
        per_device,
        mesh=mesh,
        in_specs=(
            P("dom", None),
            P(None, None, "head"),
            P(),
            P(None, "head"),
            P("head", None),
            P(),
            P(),
            P("dom", None),
            P("dom", None, None),
            P("dom", None),
            P(None, "dom", None),
            P("dom"),
        ),
        out_specs=P(("dom", "head"), None),
        check_vma=False,
    )
```

```python
import functools

import jax
import jax.numpy as jnp
from jax import lax
from jax.experimental import pallas as pl
from jax.experimental.pallas import tpu as pltpu
from jax.sharding import PartitionSpec as P

HEAD_DIM = 16
BLOCK = 128
CHUNK = 512
MESH = pl.DeviceIdType.MESH
F32 = jnp.float32
BF16 = jnp.bfloat16
NEG = -1e30


def dot_nt(a, b):
    return lax.dot_general(a, b, (((1,), (1,)), ((), ())), preferred_element_type=F32)


def dot_nn(a, b):
    return jnp.dot(a, b, preferred_element_type=F32)


def iota(shape, dim):
    return lax.broadcasted_iota(jnp.int32, shape, dim)


def gather_rows(count, index, first, table, out, out_first):
    for u in range(count):
        out[out_first + u : out_first + u + 1, :] = table[pl.ds(index[first + u], 1), :]


def widen(source, source_base, out, out_base, rows):
    def step(i, carry):
        at = pl.multiple_of(i * 256, 256)
        out[pl.ds(out_base + at, 256), :] = source[pl.ds(source_base + at, 256), :].astype(F32)
        return carry

    lax.fori_loop(0, rows // 256, step, 0)


def layer_norm_cols(values, gain):
    count = values.shape[0]
    center = jnp.sum(values, axis=0, keepdims=True) * (1.0 / count)
    shifted = values - center
    second = jnp.sum(shifted * shifted, axis=0, keepdims=True) * (1.0 / count)
    return shifted * lax.rsqrt(second + 1e-05) * gain


def prepare(weights, wo, gains, vtab, own, wq_p, wkv_p, w1_t, w2_t, wo_t, gain_cols, q_rows, k_rows, q_t, v_t, vk_h, vv_h):
    n_head, _, width = weights.shape
    local = width // n_head
    heads = width // HEAD_DIM
    f_rows = (weights.shape[1] - 3 * local) // 2

    def whole(lo, count):
        return jnp.concatenate([weights[h, lo : lo + count, :] for h in range(n_head)], axis=0)

    row, col = iota((width, width), 0), iota((width, width), 1)
    order = (col == lax.rem(row, heads) * HEAD_DIM + row // heads).astype(BF16)
    eye = (row == col).astype(BF16)
    scale = HEAD_DIM ** (-0.5)
    wq = (dot_nn(order, whole(0, local)) * scale).astype(BF16)
    wk = dot_nn(order, whole(local, local)).astype(BF16)
    wv = dot_nn(order, whole(2 * local, local)).astype(BF16)
    wkv_p[0:width, :] = wk
    wkv_p[width : 2 * width, :] = wv
    w1_t[...] = whole(3 * local, f_rows)
    w2_t[...] = dot_nt(eye, whole(3 * local + f_rows, f_rows)).astype(BF16)
    wo_t[...] = dot_nt(eye, dot_nn(order, wo[...]).astype(BF16)).astype(BF16)
    for g in (0, 1):
        gain_cols[g] = jnp.transpose(jnp.broadcast_to(gains[g : g + 1, :], (width, width)))
    q_rows[...] = dot_nt(own, wq).astype(BF16)
    k_rows[...] = dot_nt(own, wk).astype(BF16)
    q_t[...] = dot_nt(wq, own).astype(BF16).astype(F32)
    v_t[...] = dot_nt(wv, own).astype(BF16)
    vk = dot_nt(vtab, wk).astype(BF16)
    vv = dot_nt(wv, vtab).astype(BF16)
    zero = jnp.zeros((), BF16)
    vk_h[...] = jnp.concatenate(
        [jnp.where(lax.rem(iota(vk.shape, 1), heads) == h, vk, zero) for h in range(heads)], axis=0
    )
    vv_h[...] = jnp.concatenate(
        [jnp.where(lax.rem(iota(vv.shape, 0), heads) == h, vv, zero) for h in range(heads)], axis=1
    )


def near_block(b, mask, vids, q_rows, k_rows, vk_h, probs, hub_probs, near_top, near_sum):
    width = q_rows.shape[1]
    heads = width // HEAD_DIM
    n_virt = vk_h.shape[0] // heads
    here = pl.ds(b * BLOCK, BLOCK) if isinstance(b, int) else pl.ds(pl.multiple_of(b * BLOCK, BLOCK), BLOCK)
    row, col = iota((BLOCK, BLOCK), 0), iota((BLOCK, BLOCK), 1)
    eye = (row == col).astype(BF16)
    bias = jnp.where((mask[here, :] > 0) | (row == col), 0.0, NEG).astype(BF16)
    bias_t = dot_nt(eye, bias)
    zero = jnp.zeros((), BF16)
    keys, queries = k_rows[here, :], q_rows[here, :]
    lane_h = lax.rem(iota((BLOCK, width), 1), heads)
    scores = dot_nt(
        keys, jnp.concatenate([jnp.where(lane_h == h, queries, zero) for h in range(heads)], axis=0)
    )
    hub = dot_nt(vk_h[...], queries)
    mine = vids[0:1, here] == iota((n_virt, BLOCK), 0)
    tops, sums = [], []
    for h in range(heads):
        near = scores[:, h * BLOCK : (h + 1) * BLOCK] + bias_t
        virt = jnp.where(mine, hub[h * n_virt : (h + 1) * n_virt], NEG)
        top = jnp.maximum(
            jnp.max(near, axis=0, keepdims=True), jnp.max(virt, axis=0, keepdims=True)
        )
        near = jnp.exp(near - top)
        virt = jnp.exp(virt - top)
        tops.append(top)
        sums.append(jnp.sum(near, axis=0, keepdims=True) + jnp.sum(virt, axis=0, keepdims=True))
        probs[pl.ds((b * heads + h) * BLOCK, BLOCK), :] = near.astype(BF16)
        hub_probs[pl.ds((b * heads + h) * n_virt, n_virt), :] = virt
    near_top[:, here] = jnp.concatenate(tops, axis=0)
    near_sum[:, here] = jnp.concatenate(sums, axis=0)


def near_values(b, probs, hub_probs, v_t, vv_h, near_out):
    width = v_t.shape[0]
    heads = width // HEAD_DIM
    n_virt = vv_h.shape[1] // heads
    here = pl.ds(b * BLOCK, BLOCK)
    values = v_t[:, here]
    sub_h = lax.rem(iota((width, BLOCK), 0), heads)
    zero = jnp.zeros((), BF16)
    by_head = jnp.concatenate([jnp.where(sub_h == h, values, zero) for h in range(heads)], axis=1)
    near = dot_nn(by_head, probs[pl.ds(b * heads * BLOCK, heads * BLOCK), :])
    hub = dot_nn(vv_h[...], hub_probs[pl.ds(b * heads * n_virt, heads * n_virt), :].astype(BF16))
    near_out[:, here] = near + hub


def far_chunk(c, size, row_refs, wkv_p, q_t, out, top_ref, sum_ref, attended=None):
    width = q_t.shape[0]
    heads = width // HEAD_DIM
    at = c * size
    here = pl.ds(at, size)
    split = (HEAD_DIM, heads, size)
    queries = q_t[:, here].reshape(split)
    wkv = wkv_p[...]
    scored, values = [], []
    for ref, first in row_refs:
        kv = dot_nt(wkv, ref[pl.ds(first + at, size), :].astype(BF16))
        keys = kv[0:width].astype(BF16).astype(F32).reshape(split)
        scored.append(jnp.sum(keys * queries, axis=0))
        values.append(kv[width:].reshape(split))
    before = top_ref[:, here]
    top = before
    for s in scored:
        top = jnp.maximum(top, s)
    shrink = jnp.exp(before - top)
    total = sum_ref[:, here] * shrink
    mixed = out[:, here].reshape(split) * shrink[None]
    for s, v in zip(scored, values):
        weight = jnp.exp(s - top)
        total = total + weight
        mixed = mixed + v * weight[None]
    if attended is None:
        top_ref[:, here] = top
        sum_ref[:, here] = total
        out[:, here] = mixed.reshape(width, size)
    else:
        attended[:, here] = (mixed * (1.0 / total)[None]).reshape(width, size).astype(BF16)


def ffn_chunk(c, size, own, attended, wo_t, w1_t, w2_t, gain_cols, out):
    width = attended.shape[0]
    at = c * size if isinstance(c, int) else pl.multiple_of(c * size, size)
    here = pl.ds(at, size)
    eye = (iota((width, width), 0) == iota((width, width), 1)).astype(BF16)
    gain = [jnp.concatenate([gain_cols[g]] * (size // width), axis=1) for g in (0, 1)]
    residual = dot_nt(eye, own(here)) + dot_nn(wo_t[...], attended[:, here])
    hidden = layer_norm_cols(residual, gain[0]).astype(BF16)
    inner = jax.nn.gelu(dot_nn(w1_t[...], hidden), approximate=True).astype(BF16)
    summed = layer_norm_cols(hidden.astype(F32) + dot_nn(w2_t[...], inner), gain[1])
    for k in range(size // width):
        out[pl.ds(at + k * width, width), :] = jnp.transpose(
            summed[:, k * width : (k + 1) * width]
        ).astype(BF16)


def layer_kernel(
    n_dom,
    n_head,
    feats_in,
    wqkv_in,
    wo_in,
    w1_in,
    w2_in,
    gains_in,
    vtab_in,
    mask_in,
    send_in,
    links_in,
    perm_in,
    vids_in,
    out,
    feats,
    table,
    staged,
    packed,
    weights,
    wo,
    gains,
    vtab,
    mask,
    vids,
    send_first,
    send_second,
    links,
    wanted,
    lists,
    matched,
    far,
    wq_p,
    wkv_p,
    w1_t,
    w2_t,
    wo_t,
    gain_cols,
    q_rows,
    k_rows,
    q_t,
    v_t,
    vk_h,
    vv_h,
    near_out,
    near_top,
    near_sum,
    attended,
    probs,
    hub_probs,
    local_sems,
    req_send,
    req_recv,
    list_send,
    list_recv,
    rows_send,
    rows_recv,
    w_send,
    w_recv,
    pass_send,
    pass_recv,
):
    nodes = feats.shape[0]
    part = out.shape[0]
    halo = lists.shape[0] // 2
    chunk = staged.shape[0]
    link_count = links_in.shape[0]
    dom = lax.axis_index("dom")
    head = lax.axis_index("head")
    core = lax.rem(dom, 2)
    peer = dom + 1 - 2 * core
    side = lax.rem(dom + 2 * core - 1 + n_dom, n_dom)
    levels = n_dom.bit_length() - 1
    mine = pl.ds(pl.multiple_of(head * part, part), part)

    def flipped(stride):
        bit = lax.rem(dom // (1 << stride), 2)
        return dom + (1 - 2 * bit) * (1 << stride)

    partners = [flipped(m * (levels - 1) // 2) for m in range(3)]
    others = [lax.rem(head + k, n_head) for k in range(1, n_head)]

    barrier = pltpu.get_barrier_semaphore()
    for dev in [side] + partners:
        pl.semaphore_signal(barrier, inc=1, device_id={"dom": dev}, device_id_type=MESH)
    for dev in others:
        pl.semaphore_signal(barrier, inc=1, device_id={"head": dev}, device_id_type=MESH)

    def fetch(k, src, dst):
        copy = pltpu.make_async_copy(src, dst, local_sems.at[k])
        copy.start()
        return copy

    q_rows_in, f_rows = wqkv_in.shape[0], w1_in.shape[0]
    got_feats = fetch(0, feats_in, feats)
    direct = halo // 2
    share = (halo - direct) // n_head
    got_first = [
        fetch(1, send_in.at[0, core, pl.ds(0, direct)], send_first.at[pl.ds(0, direct)]),
        fetch(
            11 + link_count,
            send_in.at[0, core, pl.ds(pl.multiple_of(direct + head * share, share), share)],
            send_first.at[pl.ds(direct, share)],
        ),
    ]
    got_second = fetch(2, send_in.at[0, 1 - core], send_second)
    got_weights = [
        fetch(3, wqkv_in, weights.at[head, pl.ds(0, q_rows_in)]),
        fetch(4, w1_in, weights.at[head, pl.ds(q_rows_in, f_rows)]),
        fetch(5, w2_in, weights.at[head, pl.ds(q_rows_in + f_rows, f_rows)]),
    ]
    got_rest = [
        fetch(6, wo_in, wo),
        fetch(7, gains_in, gains),
        fetch(8, vtab_in, vtab),
        fetch(9, mask_in.at[mine], mask),
        fetch(10, vids_in.at[:, mine], vids),
    ]
    got_links = [
        fetch(11 + e, links_in.at[e, mine], links.at[pl.ds(e * part, part)]) for e in range(link_count)
    ]

    def remote(src, dst, send, recv, device):
        return pltpu.make_async_remote_copy(
            src_ref=src, dst_ref=dst, send_sem=send, recv_sem=recv, device_id=device, device_id_type=MESH
        )

    pl.semaphore_wait(barrier, 4 + len(others))
    requests = []
    for m in range(3):
        copy = remote(
            perm_in.at[m, 0, mine], wanted.at[pl.ds(m * part, part)], req_send.at[m], req_recv.at[m], {"dom": partners[m]}
        )
        copy.start()
        requests.append(copy)
    for copy in got_weights:
        copy.wait()
    w_copies = []
    for k, dev in enumerate(others):
        copy = remote(weights.at[head], weights.at[head], w_send.at[k], w_recv.at[head], {"head": dev})
        copy.start()
        w_copies.append(copy)

    got_feats.wait()
    widen(feats, 0, table, 0, nodes)

    sent = []

    used = [0]

    def send_chunk(rows, index, first, dst, send, recv, device):
        to = packed.at[pl.ds(used[0], rows)]
        used[0] += rows
        gather_rows(rows, index, first, table, staged, 0)
        to[...] = staged[0:rows, :].astype(BF16)
        copy = remote(to, dst, send, recv, device)
        copy.start()
        sent.append(copy)
        return copy

    def shared(base, h):
        return lists.at[pl.ds(pl.multiple_of(base * halo + direct + h * share, share), share)]

    for copy in got_first:
        copy.wait()
    to_side = {"dom": side}
    quarter = send_chunk(
        share, send_first, direct, shared(1 - core, head), list_send.at[0], list_recv.at[0], to_side
    )
    list_copies = []
    for i in range(direct // chunk):
        at = pl.multiple_of((1 - core) * halo + i * chunk, chunk)
        dst = lists.at[pl.ds(at, chunk)]
        s = 1 + i
        list_copies.append(
            send_chunk(chunk, send_first, i * chunk, dst, list_send.at[s], list_recv.at[s], to_side)
        )

    pieces = part // chunk
    row_copies = {}

    def serve(m):
        requests[m].wait_recv()
        for i in range(pieces):
            s = m * pieces + i
            row_copies[m, i] = send_chunk(
                chunk,
                wanted,
                m * part + i * chunk,
                matched.at[m, pl.ds(i * chunk, chunk)],
                rows_send.at[s],
                rows_recv.at[s],
                {"dom": partners[m]},
            )

    serve(1)
    quarter.wait_recv()
    passed = []
    for k, dev in enumerate(others):
        copy = remote(
            shared(core, head), shared(core, head), pass_send.at[k], pass_recv.at[head], {"head": dev}
        )
        copy.start()
        passed.append(copy)
    serve(2)
    got_second.wait()
    for i in range(halo // chunk):
        at = pl.multiple_of(core * halo + i * chunk, chunk)
        dst = lists.at[pl.ds(at, chunk)]
        s = 1 + direct // chunk + i
        list_copies.append(
            send_chunk(
                chunk, send_second, i * chunk, dst, list_send.at[s], list_recv.at[s], {"dom": peer}
            )
        )
    serve(0)

    for dev in others:
        remote(weights.at[head], weights.at[dev], w_send.at[0], w_recv.at[dev], {"head": dev}).wait_recv()
    for copy in got_rest:
        copy.wait()
    prepare(
        weights, wo, gains, vtab[...], feats[mine, :], wq_p, wkv_p, w1_t, w2_t, wo_t, gain_cols,
        q_rows, k_rows, q_t, v_t, vk_h, vv_h,
    )
    for b in range(part // BLOCK):
        near_block(b, mask, vids, q_rows, k_rows, vk_h, probs, hub_probs, near_top, near_sum)
    for b in range(part // BLOCK):
        near_values(b, probs, hub_probs, v_t, vv_h, near_out)

    for dev in others:
        remote(
            shared(core, head), shared(core, dev), pass_send.at[0], pass_recv.at[dev], {"head": dev}
        ).wait_recv()
    for copy in list_copies:
        copy.wait_recv()
    widen(lists, 0, table, 0, 2 * halo)
    for copy in got_links:
        copy.wait()
    gather_rows(link_count * part, links, 0, table, far, 0)

    for m in (0, 2):
        for i in range(pieces):
            row_copies[m, i].wait_recv()
    row_refs = [(far, e * part) for e in range(link_count)] + [(matched.at[m], 0) for m in (0, 2)]
    for c in range(part // 256):
        far_chunk(c, 256, row_refs, wkv_p, q_t, near_out, near_top, near_sum)
    for i in range(pieces):
        row_copies[1, i].wait_recv()
    for c in range(part // 256):
        far_chunk(c, 256, [(matched.at[1], 0)], wkv_p, q_t, near_out, near_top, near_sum, attended)
    own_base = pl.multiple_of(head * part, part)
    ffn_chunk(
        0,
        part,
        lambda here: feats[pl.ds(own_base + here.start, here.size), :],
        attended,
        wo_t,
        w1_t,
        w2_t,
        gain_cols,
        out,
    )
    for copy in requests + w_copies + sent + passed:
        copy.wait_send()


def per_device(
    features,
    qkv_weight,
    out_weight,
    ffn_in,
    ffn_out,
    norm_gains,
    virtual_table,
    block_mask,
    halo_send,
    halo_links,
    expander_perm,
    virtual_ids,
):
    nodes, width = features.shape
    n_dom = lax.axis_size("dom")
    n_head = lax.axis_size("head")
    part = nodes // n_head
    halo = halo_send.shape[2]
    heads = width // HEAD_DIM
    n_virt = virtual_table.shape[0]
    wqkv = jnp.transpose(qkv_weight, (1, 2, 0)).reshape(-1, width)
    w1 = ffn_in.T
    w_rows = wqkv.shape[0] + 2 * w1.shape[0]
    hidden = n_head * w1.shape[0]
    links = halo_links.T
    link_count = links.shape[0]
    vids = virtual_ids.reshape(1, nodes)
    chunk = CHUNK
    direct = halo // 2
    share = (halo - direct) // n_head
    lists = 1 + direct // chunk + halo // chunk
    pieces = 3 * part // chunk
    i32 = jnp.int32
    dma = pltpu.SemaphoreType.DMA
    return pl.pallas_call(
        functools.partial(layer_kernel, n_dom, n_head),
        name="layer",
        out_shape=jax.ShapeDtypeStruct((part, width), BF16),
        in_specs=[pl.BlockSpec(memory_space=pl.ANY)] * 12,
        out_specs=pl.BlockSpec(memory_space=pltpu.VMEM),
        scratch_shapes=[
            pltpu.VMEM((nodes, width), BF16),
            pltpu.VMEM((nodes, width), F32),
            pltpu.VMEM((chunk, width), F32),
            pltpu.VMEM((share + direct + halo + 3 * part, width), BF16),
            pltpu.VMEM((n_head, w_rows, width), BF16),
            pltpu.VMEM((width, width), BF16),
            pltpu.VMEM((2, width), F32),
            pltpu.VMEM((n_virt, width), BF16),
            pltpu.VMEM((part, BLOCK), i32),
            pltpu.VMEM((1, part), i32),
            pltpu.SMEM((direct + share,), i32),
            pltpu.SMEM((halo,), i32),
            pltpu.SMEM((link_count * part,), i32),
            pltpu.SMEM((3 * part,), i32),
            pltpu.VMEM((2 * halo, width), BF16),
            pltpu.VMEM((3, part, width), BF16),
            pltpu.VMEM((link_count * part, width), F32),
            pltpu.VMEM((width, width), BF16),
            pltpu.VMEM((2 * width, width), BF16),
            pltpu.VMEM((hidden, width), BF16),
            pltpu.VMEM((width, hidden), BF16),
            pltpu.VMEM((width, width), BF16),
            pltpu.VMEM((2, width, width), F32),
            pltpu.VMEM((part, width), BF16),
            pltpu.VMEM((part, width), BF16),
            pltpu.VMEM((width, part), F32),
            pltpu.VMEM((width, part), BF16),
            pltpu.VMEM((heads * n_virt, width), BF16),
            pltpu.VMEM((width, heads * n_virt), BF16),
            pltpu.VMEM((width, part), F32),
            pltpu.VMEM((heads, part), F32),
            pltpu.VMEM((heads, part), F32),
            pltpu.VMEM((width, part), BF16),
            pltpu.VMEM((heads * part, BLOCK), BF16),
            pltpu.VMEM((heads * n_virt * part // BLOCK, BLOCK), F32),
            dma((12 + link_count,)),
            dma((3,)),
            dma((3,)),
            dma((lists,)),
            dma((lists,)),
            dma((pieces,)),
            dma((pieces,)),
            dma((n_head - 1,)),
            dma((n_head,)),
            dma((n_head - 1,)),
            dma((n_head,)),
        ],
        compiler_params=pltpu.CompilerParams(
            collective_id=0, has_side_effects=True, vmem_limit_bytes=60 << 20
        ),
    )(
        features,
        wqkv,
        out_weight,
        w1,
        ffn_out,
        norm_gains,
        virtual_table,
        block_mask,
        halo_send,
        links,
        expander_perm,
        vids,
    )


def solution(mesh):
    return jax.shard_map(
        per_device,
        mesh=mesh,
        in_specs=(
            P("dom", None),
            P(None, None, "head"),
            P(),
            P(None, "head"),
            P("head", None),
            P(),
            P(),
            P("dom", None),
            P("dom", None, None),
            P("dom", None),
            P(None, "dom", None),
            P("dom"),
        ),
        out_specs=P(("dom", "head"), None),
        check_vma=False,
    )
```

```python
import functools

import jax
import jax.numpy as jnp
from jax import lax
from jax.experimental import pallas as pl
from jax.experimental.pallas import tpu as pltpu
from jax.sharding import PartitionSpec as P

HEAD_DIM = 16
BLOCK = 128
CHUNK = 512
PIECE = 512
MESH = pl.DeviceIdType.MESH
F32 = jnp.float32
BF16 = jnp.bfloat16
NEG = -1e30


def dot_nt(a, b):
    return lax.dot_general(a, b, (((1,), (1,)), ((), ())), preferred_element_type=F32)


def dot_nn(a, b):
    return jnp.dot(a, b, preferred_element_type=F32)


def iota(shape, dim):
    return lax.broadcasted_iota(jnp.int32, shape, dim)


def gather_rows(count, index, first, table, out, out_first):
    for u in range(count):
        out[out_first + u : out_first + u + 1, :] = table[pl.ds(index[first + u], 1), :]


def widen(source, source_base, out, out_base, rows):
    def step(i, carry):
        at = pl.multiple_of(i * 256, 256)
        out[pl.ds(out_base + at, 256), :] = source[pl.ds(source_base + at, 256), :].astype(F32)
        return carry

    lax.fori_loop(0, rows // 256, step, 0)


def layer_norm_cols(values, gain):
    count = values.shape[0]
    center = jnp.sum(values, axis=0, keepdims=True) * (1.0 / count)
    shifted = values - center
    second = jnp.sum(shifted * shifted, axis=0, keepdims=True) * (1.0 / count)
    return shifted * lax.rsqrt(second + 1e-05) * gain


def prepare(weights, wo, gains, vtab, own, wq_p, wkv_p, w1_t, w2_t, wo_t, gain_cols, q_rows, k_rows, q_t, own_t, v_t, vk_h, vv_h):
    n_head, _, width = weights.shape
    local = width // n_head
    heads = width // HEAD_DIM
    f_rows = (weights.shape[1] - 3 * local) // 2

    def whole(lo, count):
        return jnp.concatenate([weights[h, lo : lo + count, :] for h in range(n_head)], axis=0)

    row, col = iota((width, width), 0), iota((width, width), 1)
    order = (col == lax.rem(row, heads) * HEAD_DIM + row // heads).astype(BF16)
    eye = (row == col).astype(BF16)
    scale = HEAD_DIM ** (-0.5)
    wq = (dot_nn(order, whole(0, local)) * scale).astype(BF16)
    wk = dot_nn(order, whole(local, local)).astype(BF16)
    wv = dot_nn(order, whole(2 * local, local)).astype(BF16)
    wkv_p[0:width, :] = wk
    wkv_p[width : 2 * width, :] = wv
    w1_t[...] = whole(3 * local, f_rows)
    w2_t[...] = dot_nt(eye, whole(3 * local + f_rows, f_rows)).astype(BF16)
    wo_t[...] = dot_nt(eye, dot_nn(order, wo[...]).astype(BF16)).astype(BF16)
    for g in (0, 1):
        gain_cols[g] = jnp.transpose(jnp.broadcast_to(gains[g : g + 1, :], (width, width)))
    q_rows[...] = dot_nt(own, wq).astype(BF16)
    k_rows[...] = dot_nt(own, wk).astype(BF16)
    q_t[...] = dot_nt(wq, own).astype(BF16).astype(F32)
    own_t[...] = dot_nt(eye, own)
    v_t[...] = dot_nt(wv, own).astype(BF16)
    vk = dot_nt(vtab, wk).astype(BF16)
    vv = dot_nt(wv, vtab).astype(BF16)
    zero = jnp.zeros((), BF16)
    vk_h[...] = jnp.concatenate(
        [jnp.where(lax.rem(iota(vk.shape, 1), heads) == h, vk, zero) for h in range(heads)], axis=0
    )
    vv_h[...] = jnp.concatenate(
        [jnp.where(lax.rem(iota(vv.shape, 0), heads) == h, vv, zero) for h in range(heads)], axis=1
    )


def near_block(b, mask, vids, q_rows, k_rows, vk_h, probs, hub_probs, near_top, near_sum):
    width = q_rows.shape[1]
    heads = width // HEAD_DIM
    n_virt = vk_h.shape[0] // heads
    here = pl.ds(b * BLOCK, BLOCK) if isinstance(b, int) else pl.ds(pl.multiple_of(b * BLOCK, BLOCK), BLOCK)
    row, col = iota((BLOCK, BLOCK), 0), iota((BLOCK, BLOCK), 1)
    eye = (row == col).astype(BF16)
    bias = jnp.where((mask[here, :] > 0) | (row == col), 0.0, NEG).astype(BF16)
    bias_t = dot_nt(eye, bias)
    zero = jnp.zeros((), BF16)
    keys, queries = k_rows[here, :], q_rows[here, :]
    lane_h = lax.rem(iota((BLOCK, width), 1), heads)
    scores = dot_nt(
        keys, jnp.concatenate([jnp.where(lane_h == h, queries, zero) for h in range(heads)], axis=0)
    )
    hub = dot_nt(vk_h[...], queries)
    mine = vids[0:1, here] == iota((n_virt, BLOCK), 0)
    tops, sums = [], []
    for h in range(heads):
        near = scores[:, h * BLOCK : (h + 1) * BLOCK] + bias_t
        virt = jnp.where(mine, hub[h * n_virt : (h + 1) * n_virt], NEG)
        top = jnp.maximum(
            jnp.max(near, axis=0, keepdims=True), jnp.max(virt, axis=0, keepdims=True)
        )
        near = jnp.exp(near - top)
        virt = jnp.exp(virt - top)
        tops.append(top)
        sums.append(jnp.sum(near, axis=0, keepdims=True) + jnp.sum(virt, axis=0, keepdims=True))
        probs[pl.ds((b * heads + h) * BLOCK, BLOCK), :] = near.astype(BF16)
        hub_probs[pl.ds((b * heads + h) * n_virt, n_virt), :] = virt
    near_top[:, here] = jnp.concatenate(tops, axis=0)
    near_sum[:, here] = jnp.concatenate(sums, axis=0)


def near_values(b, probs, hub_probs, v_t, vv_h, near_out):
    width = v_t.shape[0]
    heads = width // HEAD_DIM
    n_virt = vv_h.shape[1] // heads
    here = pl.ds(b * BLOCK, BLOCK)
    values = v_t[:, here]
    sub_h = lax.rem(iota((width, BLOCK), 0), heads)
    zero = jnp.zeros((), BF16)
    by_head = jnp.concatenate([jnp.where(sub_h == h, values, zero) for h in range(heads)], axis=1)
    near = dot_nn(by_head, probs[pl.ds(b * heads * BLOCK, heads * BLOCK), :])
    hub = dot_nn(vv_h[...], hub_probs[pl.ds(b * heads * n_virt, heads * n_virt), :].astype(BF16))
    near_out[:, here] = near + hub


def far_chunk(c, size, row_refs, wkv_p, q_t, out, top_ref, sum_ref, attended=None):
    width = q_t.shape[0]
    heads = width // HEAD_DIM
    at = c * size
    here = pl.ds(at, size)
    split = (HEAD_DIM, heads, size)
    queries = q_t[:, here].reshape(split)
    wkv = wkv_p[...]
    scored, values = [], []
    for ref, first in row_refs:
        kv = dot_nt(wkv, ref[pl.ds(first + at, size), :].astype(BF16))
        keys = kv[0:width].astype(BF16).astype(F32).reshape(split)
        scored.append(jnp.sum(keys * queries, axis=0))
        values.append(kv[width:].reshape(split))
    before = top_ref[:, here]
    top = before
    for s in scored:
        top = jnp.maximum(top, s)
    shrink = jnp.exp(before - top)
    total = sum_ref[:, here] * shrink
    mixed = out[:, here].reshape(split) * shrink[None]
    for s, v in zip(scored, values):
        weight = jnp.exp(s - top)
        total = total + weight
        mixed = mixed + v * weight[None]
    if attended is None:
        top_ref[:, here] = top
        sum_ref[:, here] = total
        out[:, here] = mixed.reshape(width, size)
    else:
        attended[:, here] = (mixed * (1.0 / total)[None]).reshape(width, size).astype(BF16)


def ffn_chunk(c, size, own_t, attended, wo_t, w1_t, w2_t, gain_cols, out):
    width = attended.shape[0]
    at = c * size if isinstance(c, int) else pl.multiple_of(c * size, size)
    here = pl.ds(at, size)
    gain = [jnp.concatenate([gain_cols[g]] * (size // width), axis=1) for g in (0, 1)]
    residual = own_t[:, here] + dot_nn(wo_t[...], attended[:, here])
    hidden = layer_norm_cols(residual, gain[0]).astype(BF16)
    inner = jax.nn.gelu(dot_nn(w1_t[...], hidden), approximate=True).astype(BF16)
    summed = layer_norm_cols(hidden.astype(F32) + dot_nn(w2_t[...], inner), gain[1])
    for k in range(size // width):
        out[pl.ds(at + k * width, width), :] = jnp.transpose(
            summed[:, k * width : (k + 1) * width]
        ).astype(BF16)


def layer_kernel(
    n_dom,
    n_head,
    feats_in,
    wqkv_in,
    wo_in,
    w1_in,
    w2_in,
    gains_in,
    vtab_in,
    mask_in,
    send_in,
    links_in,
    perm_in,
    vids_in,
    out,
    feats,
    table,
    staged,
    packed,
    weights,
    wo,
    gains,
    vtab,
    mask,
    vids,
    send_first,
    send_second,
    links,
    wanted,
    lists,
    matched,
    far,
    wq_p,
    wkv_p,
    w1_t,
    w2_t,
    wo_t,
    gain_cols,
    q_rows,
    k_rows,
    q_t,
    own_t,
    v_t,
    vk_h,
    vv_h,
    near_out,
    near_top,
    near_sum,
    attended,
    probs,
    hub_probs,
    local_sems,
    req_send,
    req_recv,
    list_send,
    list_recv,
    rows_send,
    rows_recv,
    w_send,
    w_recv,
    pass_send,
    pass_recv,
):
    nodes = feats.shape[0]
    part = out.shape[0]
    halo = lists.shape[0] // 2
    chunk = staged.shape[0]
    link_count = links_in.shape[0]
    dom = lax.axis_index("dom")
    head = lax.axis_index("head")
    core = lax.rem(dom, 2)
    peer = dom + 1 - 2 * core
    side = lax.rem(dom + 2 * core - 1 + n_dom, n_dom)
    levels = n_dom.bit_length() - 1
    mine = pl.ds(pl.multiple_of(head * part, part), part)

    def flipped(stride):
        bit = lax.rem(dom // (1 << stride), 2)
        return dom + (1 - 2 * bit) * (1 << stride)

    partners = [flipped(m * (levels - 1) // 2) for m in range(3)]
    others = [lax.rem(head + k, n_head) for k in range(1, n_head)]

    barrier = pltpu.get_barrier_semaphore()
    for dev in [side] + partners:
        pl.semaphore_signal(barrier, inc=1, device_id={"dom": dev}, device_id_type=MESH)
    for dev in others:
        pl.semaphore_signal(barrier, inc=1, device_id={"head": dev}, device_id_type=MESH)

    def fetch(k, src, dst):
        copy = pltpu.make_async_copy(src, dst, local_sems.at[k])
        copy.start()
        return copy

    q_rows_in, f_rows = wqkv_in.shape[0], w1_in.shape[0]
    got_feats = fetch(0, feats_in, feats)
    direct = halo // 4
    share = (halo - direct) // n_head
    got_first = [
        fetch(1, send_in.at[0, core, pl.ds(0, direct)], send_first.at[pl.ds(0, direct)]),
        fetch(
            11 + link_count,
            send_in.at[0, core, pl.ds(pl.multiple_of(direct + head * share, 128), share)],
            send_first.at[pl.ds(direct, share)],
        ),
    ]
    got_second = fetch(2, send_in.at[0, 1 - core], send_second)
    got_weights = [
        fetch(3, wqkv_in, weights.at[head, pl.ds(0, q_rows_in)]),
        fetch(4, w1_in, weights.at[head, pl.ds(q_rows_in, f_rows)]),
        fetch(5, w2_in, weights.at[head, pl.ds(q_rows_in + f_rows, f_rows)]),
    ]
    got_rest = [
        fetch(6, wo_in, wo),
        fetch(7, gains_in, gains),
        fetch(8, vtab_in, vtab),
        fetch(9, mask_in.at[mine], mask),
        fetch(10, vids_in.at[:, mine], vids),
    ]
    got_links = [
        fetch(11 + e, links_in.at[e, mine], links.at[pl.ds(e * part, part)]) for e in range(link_count)
    ]

    def remote(src, dst, send, recv, device):
        return pltpu.make_async_remote_copy(
            src_ref=src, dst_ref=dst, send_sem=send, recv_sem=recv, device_id=device, device_id_type=MESH
        )

    pl.semaphore_wait(barrier, 4 + len(others))
    requests = []
    for m in range(3):
        copy = remote(
            perm_in.at[m, 0, mine], wanted.at[pl.ds(m * part, part)], req_send.at[m], req_recv.at[m], {"dom": partners[m]}
        )
        copy.start()
        requests.append(copy)
    for copy in got_weights:
        copy.wait()
    w_copies = []
    for k, dev in enumerate(others):
        copy = remote(weights.at[head], weights.at[head], w_send.at[k], w_recv.at[head], {"head": dev})
        copy.start()
        w_copies.append(copy)

    got_feats.wait()
    widen(feats, 0, table, 0, nodes)

    sent = []

    used = [0]

    def send_chunk(rows, index, first, dst, send, recv, device):
        to = packed.at[pl.ds(used[0], rows)]
        used[0] += rows
        gather_rows(rows, index, first, table, staged, 0)
        to[...] = staged[0:rows, :].astype(BF16)
        copy = remote(to, dst, send, recv, device)
        copy.start()
        sent.append(copy)
        return copy

    def shared(base, h):
        return lists.at[pl.ds(pl.multiple_of(base * halo + direct + h * share, 128), share)]

    for copy in got_first:
        copy.wait()
    to_side = {"dom": side}
    quarter = send_chunk(
        share, send_first, direct, shared(1 - core, head), list_send.at[0], list_recv.at[0], to_side
    )
    list_copies = []
    for i in range(direct // chunk):
        at = pl.multiple_of((1 - core) * halo + i * chunk, chunk)
        dst = lists.at[pl.ds(at, chunk)]
        s = 1 + i
        list_copies.append(
            send_chunk(chunk, send_first, i * chunk, dst, list_send.at[s], list_recv.at[s], to_side)
        )

    pieces = part // PIECE
    row_copies = {}

    def serve(m, i):
        if i == 0:
            requests[m].wait_recv()
        s = m * pieces + i
        row_copies[m, i] = send_chunk(
            PIECE,
            wanted,
            m * part + i * PIECE,
            matched.at[m, pl.ds(i * PIECE, PIECE)],
            rows_send.at[s],
            rows_recv.at[s],
            {"dom": partners[m]},
        )

    got_second.wait()
    for i in range(halo // chunk):
        at = pl.multiple_of(core * halo + i * chunk, chunk)
        dst = lists.at[pl.ds(at, chunk)]
        s = 1 + direct // chunk + i
        list_copies.append(
            send_chunk(
                chunk, send_second, i * chunk, dst, list_send.at[s], list_recv.at[s], {"dom": peer}
            )
        )

    serve(1, 0)
    serve(2, 0)
    quarter.wait_recv()
    passed = []
    for k, dev in enumerate(others):
        copy = remote(
            shared(core, head), shared(core, head), pass_send.at[k], pass_recv.at[head], {"head": dev}
        )
        copy.start()
        passed.append(copy)
    for i in range(1, pieces):
        serve(1, i)
        serve(2, i)
    for i in range(pieces):
        serve(0, i)

    for dev in others:
        remote(weights.at[head], weights.at[dev], w_send.at[0], w_recv.at[dev], {"head": dev}).wait_recv()
    for copy in got_rest:
        copy.wait()
    prepare(
        weights, wo, gains, vtab[...], feats[mine, :], wq_p, wkv_p, w1_t, w2_t, wo_t, gain_cols,
        q_rows, k_rows, q_t, own_t, v_t, vk_h, vv_h,
    )
    for b in range(part // BLOCK):
        near_block(b, mask, vids, q_rows, k_rows, vk_h, probs, hub_probs, near_top, near_sum)
    for b in range(part // BLOCK):
        near_values(b, probs, hub_probs, v_t, vv_h, near_out)

    for copy in list_copies:
        copy.wait_recv()
    from_peer = pl.multiple_of((1 - core) * halo, halo)
    from_side = pl.multiple_of(core * halo, halo)
    widen(lists, from_peer, table, from_peer, halo)
    widen(lists, from_side, table, from_side, direct)
    for dev in others:
        remote(
            shared(core, head), shared(core, dev), pass_send.at[0], pass_recv.at[dev], {"head": dev}
        ).wait_recv()
    passed_on = pl.multiple_of(core * halo + direct, chunk)
    widen(lists, passed_on, table, passed_on, halo - direct)
    for copy in got_links:
        copy.wait()
    gather_rows(link_count * part, links, 0, table, far, 0)

    for i in range(pieces):
        row_copies[0, i].wait_recv()
    row_refs = [(far, e * part) for e in range(link_count)] + [(matched.at[0], 0)]
    for c in range(part // 256):
        far_chunk(c, 256, row_refs, wkv_p, q_t, near_out, near_top, near_sum)
    for m in (2, 1):
        for i in range(pieces):
            row_copies[m, i].wait_recv()
    row_refs = [(matched.at[m], 0) for m in (1, 2)]
    for c in range(part // 256):
        far_chunk(c, 256, row_refs, wkv_p, q_t, near_out, near_top, near_sum, attended)
    ffn_chunk(
        0,
        part,
        own_t,
        attended,
        wo_t,
        w1_t,
        w2_t,
        gain_cols,
        out,
    )
    for copy in requests + w_copies + sent + passed:
        copy.wait_send()


def per_device(
    features,
    qkv_weight,
    out_weight,
    ffn_in,
    ffn_out,
    norm_gains,
    virtual_table,
    block_mask,
    halo_send,
    halo_links,
    expander_perm,
    virtual_ids,
):
    nodes, width = features.shape
    n_dom = lax.axis_size("dom")
    n_head = lax.axis_size("head")
    part = nodes // n_head
    halo = halo_send.shape[2]
    heads = width // HEAD_DIM
    n_virt = virtual_table.shape[0]
    wqkv = jnp.transpose(qkv_weight, (1, 2, 0)).reshape(-1, width)
    w1 = ffn_in.T
    w_rows = wqkv.shape[0] + 2 * w1.shape[0]
    hidden = n_head * w1.shape[0]
    links = halo_links.T
    link_count = links.shape[0]
    vids = virtual_ids.reshape(1, nodes)
    chunk = CHUNK
    direct = halo // 4
    share = (halo - direct) // n_head
    lists = 1 + direct // chunk + halo // chunk
    pieces = 3 * part // PIECE
    i32 = jnp.int32
    dma = pltpu.SemaphoreType.DMA
    return pl.pallas_call(
        functools.partial(layer_kernel, n_dom, n_head),
        name="layer",
        out_shape=jax.ShapeDtypeStruct((part, width), BF16),
        in_specs=[pl.BlockSpec(memory_space=pl.ANY)] * 12,
        out_specs=pl.BlockSpec(memory_space=pltpu.VMEM),
        scratch_shapes=[
            pltpu.VMEM((nodes, width), BF16),
            pltpu.VMEM((nodes, width), F32),
            pltpu.VMEM((chunk, width), F32),
            pltpu.VMEM((share + direct + halo + 3 * part, width), BF16),
            pltpu.VMEM((n_head, w_rows, width), BF16),
            pltpu.VMEM((width, width), BF16),
            pltpu.VMEM((2, width), F32),
            pltpu.VMEM((n_virt, width), BF16),
            pltpu.VMEM((part, BLOCK), i32),
            pltpu.VMEM((1, part), i32),
            pltpu.SMEM((direct + share,), i32),
            pltpu.SMEM((halo,), i32),
            pltpu.SMEM((link_count * part,), i32),
            pltpu.SMEM((3 * part,), i32),
            pltpu.VMEM((2 * halo, width), BF16),
            pltpu.VMEM((3, part, width), BF16),
            pltpu.VMEM((link_count * part, width), F32),
            pltpu.VMEM((width, width), BF16),
            pltpu.VMEM((2 * width, width), BF16),
            pltpu.VMEM((hidden, width), BF16),
            pltpu.VMEM((width, hidden), BF16),
            pltpu.VMEM((width, width), BF16),
            pltpu.VMEM((2, width, width), F32),
            pltpu.VMEM((part, width), BF16),
            pltpu.VMEM((part, width), BF16),
            pltpu.VMEM((width, part), F32),
            pltpu.VMEM((width, part), F32),
            pltpu.VMEM((width, part), BF16),
            pltpu.VMEM((heads * n_virt, width), BF16),
            pltpu.VMEM((width, heads * n_virt), BF16),
            pltpu.VMEM((width, part), F32),
            pltpu.VMEM((heads, part), F32),
            pltpu.VMEM((heads, part), F32),
            pltpu.VMEM((width, part), BF16),
            pltpu.VMEM((heads * part, BLOCK), BF16),
            pltpu.VMEM((heads * n_virt * part // BLOCK, BLOCK), F32),
            dma((12 + link_count,)),
            dma((3,)),
            dma((3,)),
            dma((lists,)),
            dma((lists,)),
            dma((pieces,)),
            dma((pieces,)),
            dma((n_head - 1,)),
            dma((n_head,)),
            dma((n_head - 1,)),
            dma((n_head,)),
        ],
        compiler_params=pltpu.CompilerParams(
            collective_id=0, has_side_effects=True, vmem_limit_bytes=60 << 20
        ),
    )(
        features,
        wqkv,
        out_weight,
        w1,
        ffn_out,
        norm_gains,
        virtual_table,
        block_mask,
        halo_send,
        links,
        expander_perm,
        vids,
    )


def solution(mesh):
    return jax.shard_map(
        per_device,
        mesh=mesh,
        in_specs=(
            P("dom", None),
            P(None, None, "head"),
            P(),
            P(None, "head"),
            P("head", None),
            P(),
            P(),
            P("dom", None),
            P("dom", None, None),
            P("dom", None),
            P(None, "dom", None),
            P("dom"),
        ),
        out_specs=P(("dom", "head"), None),
        check_vma=False,
    )
```

```python
import functools

import jax
import jax.numpy as jnp
from jax import lax
from jax.experimental import pallas as pl
from jax.experimental.pallas import tpu as pltpu
from jax.sharding import PartitionSpec as P

HEAD_DIM = 16
BLOCK = 128
CHUNK = 512
PIECE = 512
MESH = pl.DeviceIdType.MESH
F32 = jnp.float32
BF16 = jnp.bfloat16
NEG = -1e30


def dot_nt(a, b):
    return lax.dot_general(a, b, (((1,), (1,)), ((), ())), preferred_element_type=F32)


def dot_nn(a, b):
    return jnp.dot(a, b, preferred_element_type=F32)


def iota(shape, dim):
    return lax.broadcasted_iota(jnp.int32, shape, dim)


def gather_rows(count, index, first, table, out, out_first):
    for u in range(count):
        out[out_first + u : out_first + u + 1, :] = table[pl.ds(index[first + u], 1), :]


def widen(source, source_base, out, out_base, rows):
    def step(i, carry):
        at = pl.multiple_of(i * 256, 256)
        out[pl.ds(out_base + at, 256), :] = source[pl.ds(source_base + at, 256), :].astype(F32)
        return carry

    lax.fori_loop(0, rows // 256, step, 0)


def layer_norm_cols(values, gain):
    count = values.shape[0]
    center = jnp.sum(values, axis=0, keepdims=True) * (1.0 / count)
    shifted = values - center
    second = jnp.sum(shifted * shifted, axis=0, keepdims=True) * (1.0 / count)
    return shifted * lax.rsqrt(second + 1e-05) * gain


def prepare(weights, wo, gains, vtab, own, wq_p, wkv_p, w1_t, w2_t, wo_t, gain_cols, q_rows, k_rows, q_t, own_t, v_t, vk_h, vv_h):
    n_head, _, width = weights.shape
    local = width // n_head
    heads = width // HEAD_DIM
    f_rows = (weights.shape[1] - 3 * local) // 2

    def whole(lo, count):
        return jnp.concatenate([weights[h, lo : lo + count, :] for h in range(n_head)], axis=0)

    row, col = iota((width, width), 0), iota((width, width), 1)
    order = (col == lax.rem(row, heads) * HEAD_DIM + row // heads).astype(BF16)
    eye = (row == col).astype(BF16)
    scale = HEAD_DIM ** (-0.5)
    wq = (dot_nn(order, whole(0, local)) * scale).astype(BF16)
    wk = dot_nn(order, whole(local, local)).astype(BF16)
    wv = dot_nn(order, whole(2 * local, local)).astype(BF16)
    wkv_p[0:width, :] = wk
    wkv_p[width : 2 * width, :] = wv
    w1_t[...] = whole(3 * local, f_rows)
    w2_t[...] = dot_nt(eye, whole(3 * local + f_rows, f_rows)).astype(BF16)
    wo_t[...] = dot_nt(eye, dot_nn(order, wo[...]).astype(BF16)).astype(BF16)
    for g in (0, 1):
        gain_cols[g] = jnp.transpose(jnp.broadcast_to(gains[g : g + 1, :], (width, width)))
    q_rows[...] = dot_nt(own, wq).astype(BF16)
    k_rows[...] = dot_nt(own, wk).astype(BF16)
    q_t[...] = dot_nt(wq, own).astype(BF16).astype(F32)
    own_t[...] = dot_nt(eye, own)
    v_t[...] = dot_nt(wv, own).astype(BF16)
    vk = dot_nt(vtab, wk).astype(BF16)
    vv = dot_nt(wv, vtab).astype(BF16)
    zero = jnp.zeros((), BF16)
    vk_h[...] = jnp.concatenate(
        [jnp.where(lax.rem(iota(vk.shape, 1), heads) == h, vk, zero) for h in range(heads)], axis=0
    )
    vv_h[...] = jnp.concatenate(
        [jnp.where(lax.rem(iota(vv.shape, 0), heads) == h, vv, zero) for h in range(heads)], axis=1
    )


def near_block(b, mask, vids, q_rows, k_rows, vk_h, probs, hub_probs, near_top, near_sum):
    width = q_rows.shape[1]
    heads = width // HEAD_DIM
    n_virt = vk_h.shape[0] // heads
    here = pl.ds(b * BLOCK, BLOCK) if isinstance(b, int) else pl.ds(pl.multiple_of(b * BLOCK, BLOCK), BLOCK)
    row, col = iota((BLOCK, BLOCK), 0), iota((BLOCK, BLOCK), 1)
    eye = (row == col).astype(BF16)
    bias = jnp.where((mask[here, :] > 0) | (row == col), 0.0, NEG).astype(BF16)
    bias_t = dot_nt(eye, bias)
    zero = jnp.zeros((), BF16)
    keys, queries = k_rows[here, :], q_rows[here, :]
    lane_h = lax.rem(iota((BLOCK, width), 1), heads)
    scores = dot_nt(
        keys, jnp.concatenate([jnp.where(lane_h == h, queries, zero) for h in range(heads)], axis=0)
    )
    hub = dot_nt(vk_h[...], queries)
    mine = vids[0:1, here] == iota((n_virt, BLOCK), 0)
    tops, sums = [], []
    for h in range(heads):
        near = scores[:, h * BLOCK : (h + 1) * BLOCK] + bias_t
        virt = jnp.where(mine, hub[h * n_virt : (h + 1) * n_virt], NEG)
        top = jnp.maximum(
            jnp.max(near, axis=0, keepdims=True), jnp.max(virt, axis=0, keepdims=True)
        )
        near = jnp.exp(near - top)
        virt = jnp.exp(virt - top)
        tops.append(top)
        sums.append(jnp.sum(near, axis=0, keepdims=True) + jnp.sum(virt, axis=0, keepdims=True))
        probs[pl.ds((b * heads + h) * BLOCK, BLOCK), :] = near.astype(BF16)
        hub_probs[pl.ds((b * heads + h) * n_virt, n_virt), :] = virt
    near_top[:, here] = jnp.concatenate(tops, axis=0)
    near_sum[:, here] = jnp.concatenate(sums, axis=0)


def near_values(b, probs, hub_probs, v_t, vv_h, near_out):
    width = v_t.shape[0]
    heads = width // HEAD_DIM
    n_virt = vv_h.shape[1] // heads
    here = pl.ds(b * BLOCK, BLOCK)
    values = v_t[:, here]
    sub_h = lax.rem(iota((width, BLOCK), 0), heads)
    zero = jnp.zeros((), BF16)
    by_head = jnp.concatenate([jnp.where(sub_h == h, values, zero) for h in range(heads)], axis=1)
    near = dot_nn(by_head, probs[pl.ds(b * heads * BLOCK, heads * BLOCK), :])
    hub = dot_nn(vv_h[...], hub_probs[pl.ds(b * heads * n_virt, heads * n_virt), :].astype(BF16))
    near_out[:, here] = near + hub


def far_chunk(c, size, row_refs, wkv_p, q_t, out, top_ref, sum_ref, attended=None):
    width = q_t.shape[0]
    heads = width // HEAD_DIM
    at = c * size
    here = pl.ds(at, size)
    split = (HEAD_DIM, heads, size)
    queries = q_t[:, here].reshape(split)
    wkv = wkv_p[...]
    scored, values = [], []
    for ref, first in row_refs:
        kv = dot_nt(wkv, ref[pl.ds(first + at, size), :].astype(BF16))
        keys = kv[0:width].astype(BF16).astype(F32).reshape(split)
        scored.append(jnp.sum(keys * queries, axis=0))
        values.append(kv[width:].reshape(split))
    before = top_ref[:, here]
    top = before
    for s in scored:
        top = jnp.maximum(top, s)
    shrink = jnp.exp(before - top)
    total = sum_ref[:, here] * shrink
    mixed = out[:, here].reshape(split) * shrink[None]
    for s, v in zip(scored, values):
        weight = jnp.exp(s - top)
        total = total + weight
        mixed = mixed + v * weight[None]
    if attended is None:
        top_ref[:, here] = top
        sum_ref[:, here] = total
        out[:, here] = mixed.reshape(width, size)
    else:
        attended[:, here] = (mixed * (1.0 / total)[None]).reshape(width, size).astype(BF16)


def ffn_chunk(c, size, own_t, attended, wo_t, w1_t, w2_t, gain_cols, out):
    width = attended.shape[0]
    at = c * size if isinstance(c, int) else pl.multiple_of(c * size, size)
    here = pl.ds(at, size)
    gain = [jnp.concatenate([gain_cols[g]] * (size // width), axis=1) for g in (0, 1)]
    residual = own_t[:, here] + dot_nn(wo_t[...], attended[:, here])
    hidden = layer_norm_cols(residual, gain[0]).astype(BF16)
    inner = jax.nn.gelu(dot_nn(w1_t[...], hidden), approximate=True).astype(BF16)
    summed = layer_norm_cols(hidden.astype(F32) + dot_nn(w2_t[...], inner), gain[1])
    for k in range(size // width):
        out[pl.ds(at + k * width, width), :] = jnp.transpose(
            summed[:, k * width : (k + 1) * width]
        ).astype(BF16)


def layer_kernel(
    n_dom,
    n_head,
    feats_in,
    wqkv_in,
    wo_in,
    w1_in,
    w2_in,
    gains_in,
    vtab_in,
    mask_in,
    send_in,
    links_in,
    perm_in,
    vids_in,
    out,
    feats,
    table,
    staged,
    packed,
    weights,
    wo,
    gains,
    vtab,
    mask,
    vids,
    send_first,
    send_second,
    links,
    wanted,
    lists,
    matched,
    far,
    wq_p,
    wkv_p,
    w1_t,
    w2_t,
    wo_t,
    gain_cols,
    q_rows,
    k_rows,
    q_t,
    own_t,
    v_t,
    vk_h,
    vv_h,
    near_out,
    near_top,
    near_sum,
    attended,
    probs,
    hub_probs,
    local_sems,
    req_send,
    req_recv,
    list_send,
    list_recv,
    rows_send,
    rows_recv,
    w_send,
    w_recv,
    pass_send,
    pass_recv,
):
    nodes = feats.shape[0]
    part = out.shape[0]
    halo = lists.shape[0] // 2
    chunk = staged.shape[0]
    link_count = links_in.shape[0]
    dom = lax.axis_index("dom")
    head = lax.axis_index("head")
    core = lax.rem(dom, 2)
    peer = dom + 1 - 2 * core
    side = lax.rem(dom + 2 * core - 1 + n_dom, n_dom)
    levels = n_dom.bit_length() - 1
    mine = pl.ds(pl.multiple_of(head * part, part), part)

    def flipped(stride):
        bit = lax.rem(dom // (1 << stride), 2)
        return dom + (1 - 2 * bit) * (1 << stride)

    partners = [flipped(m * (levels - 1) // 2) for m in range(3)]
    others = [lax.rem(head + k, n_head) for k in range(1, n_head)]

    barrier = pltpu.get_barrier_semaphore()
    for dev in [side] + partners:
        pl.semaphore_signal(barrier, inc=1, device_id={"dom": dev}, device_id_type=MESH)
    for dev in others:
        pl.semaphore_signal(barrier, inc=1, device_id={"head": dev}, device_id_type=MESH)

    def fetch(k, src, dst):
        copy = pltpu.make_async_copy(src, dst, local_sems.at[k])
        copy.start()
        return copy

    q_rows_in, f_rows = wqkv_in.shape[0], w1_in.shape[0]
    got_feats = fetch(0, feats_in, feats)
    direct = halo // 4
    share = (halo - direct) // n_head
    got_first = [
        fetch(1, send_in.at[0, core, pl.ds(0, direct)], send_first.at[pl.ds(0, direct)]),
        fetch(
            11 + link_count,
            send_in.at[0, core, pl.ds(pl.multiple_of(direct + head * share, 128), share)],
            send_first.at[pl.ds(direct, share)],
        ),
    ]
    got_second = fetch(2, send_in.at[0, 1 - core], send_second)
    got_weights = [
        fetch(3, wqkv_in, weights.at[head, pl.ds(0, q_rows_in)]),
        fetch(4, w1_in, weights.at[head, pl.ds(q_rows_in, f_rows)]),
        fetch(5, w2_in, weights.at[head, pl.ds(q_rows_in + f_rows, f_rows)]),
    ]
    def remote(src, dst, send, recv, device):
        return pltpu.make_async_remote_copy(
            src_ref=src, dst_ref=dst, send_sem=send, recv_sem=recv, device_id=device, device_id_type=MESH
        )

    pl.semaphore_wait(barrier, 4 + len(others))
    requests = {}
    for m in (1, 2, 0):
        copy = remote(
            perm_in.at[m, 0, mine], wanted.at[pl.ds(m * part, part)], req_send.at[m], req_recv.at[m], {"dom": partners[m]}
        )
        copy.start()
        requests[m] = copy
    for copy in got_weights:
        copy.wait()
    w_copies = []
    for k, dev in enumerate(others):
        copy = remote(weights.at[head], weights.at[head], w_send.at[k], w_recv.at[head], {"head": dev})
        copy.start()
        w_copies.append(copy)

    got_rest = [
        fetch(6, wo_in, wo),
        fetch(7, gains_in, gains),
        fetch(8, vtab_in, vtab),
        fetch(9, mask_in.at[mine], mask),
        fetch(10, vids_in.at[:, mine], vids),
    ]
    got_links = [
        fetch(11 + e, links_in.at[e, mine], links.at[pl.ds(e * part, part)]) for e in range(link_count)
    ]

    got_feats.wait()
    widen(feats, 0, table, 0, nodes)

    sent = []

    used = [0]

    def send_chunk(rows, index, first, dst, send, recv, device):
        to = packed.at[pl.ds(used[0], rows)]
        used[0] += rows
        gather_rows(rows, index, first, table, staged, 0)
        to[...] = staged[0:rows, :].astype(BF16)
        copy = remote(to, dst, send, recv, device)
        copy.start()
        sent.append(copy)
        return copy

    def shared(base, h):
        return lists.at[pl.ds(pl.multiple_of(base * halo + direct + h * share, 128), share)]

    for copy in got_first:
        copy.wait()
    to_side = {"dom": side}
    quarter = send_chunk(
        share, send_first, direct, shared(1 - core, head), list_send.at[0], list_recv.at[0], to_side
    )
    list_copies = []
    for i in range(direct // chunk):
        at = pl.multiple_of((1 - core) * halo + i * chunk, chunk)
        dst = lists.at[pl.ds(at, chunk)]
        s = 1 + i
        list_copies.append(
            send_chunk(chunk, send_first, i * chunk, dst, list_send.at[s], list_recv.at[s], to_side)
        )

    pieces = part // PIECE
    row_copies = {}

    def serve(m, i):
        if i == 0:
            requests[m].wait_recv()
        s = m * pieces + i
        row_copies[m, i] = send_chunk(
            PIECE,
            wanted,
            m * part + i * PIECE,
            matched.at[m, pl.ds(i * PIECE, PIECE)],
            rows_send.at[s],
            rows_recv.at[s],
            {"dom": partners[m]},
        )

    got_second.wait()
    for i in range(halo // chunk):
        at = pl.multiple_of(core * halo + i * chunk, chunk)
        dst = lists.at[pl.ds(at, chunk)]
        s = 1 + direct // chunk + i
        list_copies.append(
            send_chunk(
                chunk, send_second, i * chunk, dst, list_send.at[s], list_recv.at[s], {"dom": peer}
            )
        )

    quarter.wait_recv()
    passed = []
    for k, dev in enumerate(others):
        copy = remote(
            shared(core, head), shared(core, head), pass_send.at[k], pass_recv.at[head], {"head": dev}
        )
        copy.start()
        passed.append(copy)
    for i in range(pieces):
        serve(1, i)
        serve(2, i)
    for i in range(pieces):
        serve(0, i)

    for dev in others:
        remote(weights.at[head], weights.at[dev], w_send.at[0], w_recv.at[dev], {"head": dev}).wait_recv()
    for copy in got_rest:
        copy.wait()
    prepare(
        weights, wo, gains, vtab[...], feats[mine, :], wq_p, wkv_p, w1_t, w2_t, wo_t, gain_cols,
        q_rows, k_rows, q_t, own_t, v_t, vk_h, vv_h,
    )
    for b in range(part // BLOCK):
        near_block(b, mask, vids, q_rows, k_rows, vk_h, probs, hub_probs, near_top, near_sum)
    for b in range(part // BLOCK):
        near_values(b, probs, hub_probs, v_t, vv_h, near_out)

    for copy in list_copies:
        copy.wait_recv()
    from_peer = pl.multiple_of((1 - core) * halo, halo)
    from_side = pl.multiple_of(core * halo, halo)
    widen(lists, from_peer, table, from_peer, halo)
    widen(lists, from_side, table, from_side, direct)
    for dev in others:
        remote(
            shared(core, head), shared(core, dev), pass_send.at[0], pass_recv.at[dev], {"head": dev}
        ).wait_recv()
    passed_on = pl.multiple_of(core * halo + direct, chunk)
    widen(lists, passed_on, table, passed_on, halo - direct)
    for copy in got_links:
        copy.wait()
    gather_rows(link_count * part, links, 0, table, far, 0)

    for i in range(pieces):
        row_copies[0, i].wait_recv()
    row_refs = [(far, e * part) for e in range(link_count)] + [(matched.at[0], 0)]
    for c in range(part // 256):
        far_chunk(c, 256, row_refs, wkv_p, q_t, near_out, near_top, near_sum)
    for m in (2, 1):
        for i in range(pieces):
            row_copies[m, i].wait_recv()
    row_refs = [(matched.at[m], 0) for m in (1, 2)]
    for c in range(part // 256):
        far_chunk(c, 256, row_refs, wkv_p, q_t, near_out, near_top, near_sum, attended)
    ffn_chunk(
        0,
        part,
        own_t,
        attended,
        wo_t,
        w1_t,
        w2_t,
        gain_cols,
        out,
    )
    for copy in list(requests.values()) + w_copies + sent + passed:
        copy.wait_send()


def per_device(
    features,
    qkv_weight,
    out_weight,
    ffn_in,
    ffn_out,
    norm_gains,
    virtual_table,
    block_mask,
    halo_send,
    halo_links,
    expander_perm,
    virtual_ids,
):
    nodes, width = features.shape
    n_dom = lax.axis_size("dom")
    n_head = lax.axis_size("head")
    part = nodes // n_head
    halo = halo_send.shape[2]
    heads = width // HEAD_DIM
    n_virt = virtual_table.shape[0]
    wqkv = jnp.transpose(qkv_weight, (1, 2, 0)).reshape(-1, width)
    w1 = ffn_in.T
    w_rows = wqkv.shape[0] + 2 * w1.shape[0]
    hidden = n_head * w1.shape[0]
    links = halo_links.T
    link_count = links.shape[0]
    vids = virtual_ids.reshape(1, nodes)
    chunk = CHUNK
    direct = halo // 4
    share = (halo - direct) // n_head
    lists = 1 + direct // chunk + halo // chunk
    pieces = 3 * part // PIECE
    i32 = jnp.int32
    dma = pltpu.SemaphoreType.DMA
    return pl.pallas_call(
        functools.partial(layer_kernel, n_dom, n_head),
        name="layer",
        out_shape=jax.ShapeDtypeStruct((part, width), BF16),
        in_specs=[pl.BlockSpec(memory_space=pl.ANY)] * 12,
        out_specs=pl.BlockSpec(memory_space=pltpu.VMEM),
        scratch_shapes=[
            pltpu.VMEM((nodes, width), BF16),
            pltpu.VMEM((nodes, width), F32),
            pltpu.VMEM((chunk, width), F32),
            pltpu.VMEM((share + direct + halo + 3 * part, width), BF16),
            pltpu.VMEM((n_head, w_rows, width), BF16),
            pltpu.VMEM((width, width), BF16),
            pltpu.VMEM((2, width), F32),
            pltpu.VMEM((n_virt, width), BF16),
            pltpu.VMEM((part, BLOCK), i32),
            pltpu.VMEM((1, part), i32),
            pltpu.SMEM((direct + share,), i32),
            pltpu.SMEM((halo,), i32),
            pltpu.SMEM((link_count * part,), i32),
            pltpu.SMEM((3 * part,), i32),
            pltpu.VMEM((2 * halo, width), BF16),
            pltpu.VMEM((3, part, width), BF16),
            pltpu.VMEM((link_count * part, width), F32),
            pltpu.VMEM((width, width), BF16),
            pltpu.VMEM((2 * width, width), BF16),
            pltpu.VMEM((hidden, width), BF16),
            pltpu.VMEM((width, hidden), BF16),
            pltpu.VMEM((width, width), BF16),
            pltpu.VMEM((2, width, width), F32),
            pltpu.VMEM((part, width), BF16),
            pltpu.VMEM((part, width), BF16),
            pltpu.VMEM((width, part), F32),
            pltpu.VMEM((width, part), F32),
            pltpu.VMEM((width, part), BF16),
            pltpu.VMEM((heads * n_virt, width), BF16),
            pltpu.VMEM((width, heads * n_virt), BF16),
            pltpu.VMEM((width, part), F32),
            pltpu.VMEM((heads, part), F32),
            pltpu.VMEM((heads, part), F32),
            pltpu.VMEM((width, part), BF16),
            pltpu.VMEM((heads * part, BLOCK), BF16),
            pltpu.VMEM((heads * n_virt * part // BLOCK, BLOCK), F32),
            dma((12 + link_count,)),
            dma((3,)),
            dma((3,)),
            dma((lists,)),
            dma((lists,)),
            dma((pieces,)),
            dma((pieces,)),
            dma((n_head - 1,)),
            dma((n_head,)),
            dma((n_head - 1,)),
            dma((n_head,)),
        ],
        compiler_params=pltpu.CompilerParams(
            collective_id=0, has_side_effects=True, vmem_limit_bytes=60 << 20
        ),
    )(
        features,
        wqkv,
        out_weight,
        w1,
        ffn_out,
        norm_gains,
        virtual_table,
        block_mask,
        halo_send,
        links,
        expander_perm,
        vids,
    )


def solution(mesh):
    return jax.shard_map(
        per_device,
        mesh=mesh,
        in_specs=(
            P("dom", None),
            P(None, None, "head"),
            P(),
            P(None, "head"),
            P("head", None),
            P(),
            P(),
            P("dom", None),
            P("dom", None, None),
            P("dom", None),
            P(None, "dom", None),
            P("dom"),
        ),
        out_specs=P(("dom", "head"), None),
        check_vma=False,
    )
```

```python
import functools

import jax
import jax.numpy as jnp
from jax import lax
from jax.experimental import pallas as pl
from jax.experimental.pallas import tpu as pltpu
from jax.sharding import PartitionSpec as P

HEAD_DIM = 16
BLOCK = 128
CHUNK = 512
PIECE = 512
MESH = pl.DeviceIdType.MESH
F32 = jnp.float32
BF16 = jnp.bfloat16
NEG = -1e30


def dot_nt(a, b):
    return lax.dot_general(a, b, (((1,), (1,)), ((), ())), preferred_element_type=F32)


def dot_nn(a, b):
    return jnp.dot(a, b, preferred_element_type=F32)


def iota(shape, dim):
    return lax.broadcasted_iota(jnp.int32, shape, dim)


def gather_rows(count, index, first, table, out, out_first):
    for u in range(count):
        out[out_first + u : out_first + u + 1, :] = table[pl.ds(index[first + u], 1), :]


def widen(source, source_base, out, out_base, rows):
    def step(i, carry):
        at = pl.multiple_of(i * 256, 256)
        out[pl.ds(out_base + at, 256), :] = source[pl.ds(source_base + at, 256), :].astype(F32)
        return carry

    lax.fori_loop(0, rows // 256, step, 0)


def layer_norm_cols(values, gain):
    count = values.shape[0]
    center = jnp.sum(values, axis=0, keepdims=True) * (1.0 / count)
    shifted = values - center
    second = jnp.sum(shifted * shifted, axis=0, keepdims=True) * (1.0 / count)
    return shifted * lax.rsqrt(second + 1e-05) * gain


def prepare(weights, wo, gains, vtab, own, wq_p, wkv_p, w1_t, w2_t, wo_t, gain_cols, q_rows, k_rows, q_t, own_t, v_t, vk_h, vv_h):
    n_head, _, width = weights.shape
    local = width // n_head
    heads = width // HEAD_DIM
    f_rows = (weights.shape[1] - 3 * local) // 2

    def whole(lo, count):
        return jnp.concatenate([weights[h, lo : lo + count, :] for h in range(n_head)], axis=0)

    row, col = iota((width, width), 0), iota((width, width), 1)
    order = (col == lax.rem(row, heads) * HEAD_DIM + row // heads).astype(BF16)
    eye = (row == col).astype(BF16)
    scale = HEAD_DIM ** (-0.5)
    wq = (dot_nn(order, whole(0, local)) * scale).astype(BF16)
    wk = dot_nn(order, whole(local, local)).astype(BF16)
    wv = dot_nn(order, whole(2 * local, local)).astype(BF16)
    wkv_p[0:width, :] = wk
    wkv_p[width : 2 * width, :] = wv
    w1_t[...] = whole(3 * local, f_rows)
    w2_t[...] = dot_nt(eye, whole(3 * local + f_rows, f_rows)).astype(BF16)
    wo_t[...] = dot_nt(eye, dot_nn(order, wo[...]).astype(BF16)).astype(BF16)
    for g in (0, 1):
        gain_cols[g] = jnp.transpose(jnp.broadcast_to(gains[g : g + 1, :], (width, width)))
    q_rows[...] = dot_nt(own, wq).astype(BF16)
    k_rows[...] = dot_nt(own, wk).astype(BF16)
    q_t[...] = dot_nt(wq, own).astype(BF16).astype(F32)
    own_t[...] = dot_nt(eye, own)
    v_t[...] = dot_nt(wv, own).astype(BF16)
    vk = dot_nt(vtab, wk).astype(BF16)
    vv = dot_nt(wv, vtab).astype(BF16)
    zero = jnp.zeros((), BF16)
    vk_h[...] = jnp.concatenate(
        [jnp.where(lax.rem(iota(vk.shape, 1), heads) == h, vk, zero) for h in range(heads)], axis=0
    )
    vv_h[...] = jnp.concatenate(
        [jnp.where(lax.rem(iota(vv.shape, 0), heads) == h, vv, zero) for h in range(heads)], axis=1
    )


def near_block(b, mask, vids, q_rows, k_rows, vk_h, probs, hub_probs, near_top, near_sum):
    width = q_rows.shape[1]
    heads = width // HEAD_DIM
    n_virt = vk_h.shape[0] // heads
    here = pl.ds(b * BLOCK, BLOCK) if isinstance(b, int) else pl.ds(pl.multiple_of(b * BLOCK, BLOCK), BLOCK)
    row, col = iota((BLOCK, BLOCK), 0), iota((BLOCK, BLOCK), 1)
    eye = (row == col).astype(BF16)
    bias = jnp.where((mask[here, :] > 0) | (row == col), 0.0, NEG).astype(BF16)
    bias_t = dot_nt(eye, bias)
    zero = jnp.zeros((), BF16)
    keys, queries = k_rows[here, :], q_rows[here, :]
    lane_h = lax.rem(iota((BLOCK, width), 1), heads)
    scores = dot_nt(
        keys, jnp.concatenate([jnp.where(lane_h == h, queries, zero) for h in range(heads)], axis=0)
    )
    hub = dot_nt(vk_h[...], queries)
    mine = vids[0:1, here] == iota((n_virt, BLOCK), 0)
    tops, sums = [], []
    for h in range(heads):
        near = scores[:, h * BLOCK : (h + 1) * BLOCK] + bias_t
        virt = jnp.where(mine, hub[h * n_virt : (h + 1) * n_virt], NEG)
        top = jnp.maximum(
            jnp.max(near, axis=0, keepdims=True), jnp.max(virt, axis=0, keepdims=True)
        )
        near = jnp.exp(near - top)
        virt = jnp.exp(virt - top)
        tops.append(top)
        sums.append(jnp.sum(near, axis=0, keepdims=True) + jnp.sum(virt, axis=0, keepdims=True))
        probs[pl.ds((b * heads + h) * BLOCK, BLOCK), :] = near.astype(BF16)
        hub_probs[pl.ds((b * heads + h) * n_virt, n_virt), :] = virt
    near_top[:, here] = jnp.concatenate(tops, axis=0)
    near_sum[:, here] = jnp.concatenate(sums, axis=0)


def near_values(b, probs, hub_probs, v_t, vv_h, near_out):
    width = v_t.shape[0]
    heads = width // HEAD_DIM
    n_virt = vv_h.shape[1] // heads
    here = pl.ds(b * BLOCK, BLOCK)
    values = v_t[:, here]
    sub_h = lax.rem(iota((width, BLOCK), 0), heads)
    zero = jnp.zeros((), BF16)
    by_head = jnp.concatenate([jnp.where(sub_h == h, values, zero) for h in range(heads)], axis=1)
    near = dot_nn(by_head, probs[pl.ds(b * heads * BLOCK, heads * BLOCK), :])
    hub = dot_nn(vv_h[...], hub_probs[pl.ds(b * heads * n_virt, heads * n_virt), :].astype(BF16))
    near_out[:, here] = near + hub


def far_chunk(c, size, row_refs, wkv_p, q_t, out, top_ref, sum_ref, attended=None):
    width = q_t.shape[0]
    heads = width // HEAD_DIM
    at = c * size
    here = pl.ds(at, size)
    split = (HEAD_DIM, heads, size)
    queries = q_t[:, here].reshape(split)
    wkv = wkv_p[...]
    scored, values = [], []
    for ref, first in row_refs:
        kv = dot_nt(wkv, ref[pl.ds(first + at, size), :].astype(BF16))
        keys = kv[0:width].astype(BF16).astype(F32).reshape(split)
        scored.append(jnp.sum(keys * queries, axis=0))
        values.append(kv[width:].reshape(split))
    before = top_ref[:, here]
    top = before
    for s in scored:
        top = jnp.maximum(top, s)
    shrink = jnp.exp(before - top)
    total = sum_ref[:, here] * shrink
    mixed = out[:, here].reshape(split) * shrink[None]
    for s, v in zip(scored, values):
        weight = jnp.exp(s - top)
        total = total + weight
        mixed = mixed + v * weight[None]
    if attended is None:
        top_ref[:, here] = top
        sum_ref[:, here] = total
        out[:, here] = mixed.reshape(width, size)
    else:
        attended[:, here] = (mixed * (1.0 / total)[None]).reshape(width, size).astype(BF16)


def ffn_chunk(c, size, own_t, attended, wo_t, w1_t, w2_t, gain_cols, out):
    width = attended.shape[0]
    at = c * size if isinstance(c, int) else pl.multiple_of(c * size, size)
    here = pl.ds(at, size)
    gain = [jnp.concatenate([gain_cols[g]] * (size // width), axis=1) for g in (0, 1)]
    residual = own_t[:, here] + dot_nn(wo_t[...], attended[:, here])
    hidden = layer_norm_cols(residual, gain[0]).astype(BF16)
    inner = jax.nn.gelu(dot_nn(w1_t[...], hidden), approximate=True).astype(BF16)
    summed = layer_norm_cols(hidden.astype(F32) + dot_nn(w2_t[...], inner), gain[1])
    for k in range(size // width):
        out[pl.ds(at + k * width, width), :] = jnp.transpose(
            summed[:, k * width : (k + 1) * width]
        ).astype(BF16)


def layer_kernel(
    n_dom,
    n_head,
    feats_in,
    wqkv_in,
    wo_in,
    w1_in,
    w2_in,
    gains_in,
    vtab_in,
    mask_in,
    send_in,
    links_in,
    perm_in,
    vids_in,
    out,
    feats,
    table,
    staged,
    packed,
    weights,
    wo,
    gains,
    vtab,
    mask,
    vids,
    send_first,
    send_second,
    links,
    wanted,
    lists,
    matched,
    far,
    wq_p,
    wkv_p,
    w1_t,
    w2_t,
    wo_t,
    gain_cols,
    q_rows,
    k_rows,
    q_t,
    own_t,
    v_t,
    vk_h,
    vv_h,
    near_out,
    near_top,
    near_sum,
    attended,
    probs,
    hub_probs,
    local_sems,
    req_send,
    req_recv,
    list_send,
    list_recv,
    rows_send,
    rows_recv,
    w_send,
    w_recv,
    pass_send,
    pass_recv,
):
    nodes = feats.shape[0]
    part = out.shape[0]
    halo = lists.shape[0] // 2
    chunk = staged.shape[0]
    link_count = links_in.shape[0]
    dom = lax.axis_index("dom")
    head = lax.axis_index("head")
    core = lax.rem(dom, 2)
    peer = dom + 1 - 2 * core
    side = lax.rem(dom + 2 * core - 1 + n_dom, n_dom)
    levels = n_dom.bit_length() - 1
    mine = pl.ds(pl.multiple_of(head * part, part), part)

    def flipped(stride):
        bit = lax.rem(dom // (1 << stride), 2)
        return dom + (1 - 2 * bit) * (1 << stride)

    partners = [flipped(m * (levels - 1) // 2) for m in range(3)]
    others = [lax.rem(head + k, n_head) for k in range(1, n_head)]

    barrier = pltpu.get_barrier_semaphore()
    for dev in [side] + partners:
        pl.semaphore_signal(barrier, inc=1, device_id={"dom": dev}, device_id_type=MESH)
    for dev in others:
        pl.semaphore_signal(barrier, inc=1, device_id={"head": dev}, device_id_type=MESH)

    def fetch(k, src, dst):
        copy = pltpu.make_async_copy(src, dst, local_sems.at[k])
        copy.start()
        return copy

    q_rows_in, f_rows = wqkv_in.shape[0], w1_in.shape[0]
    got_feats = fetch(0, feats_in, feats)
    direct = halo // 4
    share = (halo - direct) // n_head
    got_first = [
        fetch(1, send_in.at[0, core, pl.ds(0, direct)], send_first.at[pl.ds(0, direct)]),
        fetch(
            11 + link_count,
            send_in.at[0, core, pl.ds(pl.multiple_of(direct + head * share, 128), share)],
            send_first.at[pl.ds(direct, share)],
        ),
    ]
    got_second = fetch(2, send_in.at[0, 1 - core], send_second)
    got_weights = [
        fetch(3, wqkv_in, weights.at[head, pl.ds(0, q_rows_in)]),
        fetch(4, w1_in, weights.at[head, pl.ds(q_rows_in, f_rows)]),
        fetch(5, w2_in, weights.at[head, pl.ds(q_rows_in + f_rows, f_rows)]),
    ]
    def remote(src, dst, send, recv, device):
        return pltpu.make_async_remote_copy(
            src_ref=src, dst_ref=dst, send_sem=send, recv_sem=recv, device_id=device, device_id_type=MESH
        )

    pl.semaphore_wait(barrier, 4 + len(others))
    requests = {}
    for m in (1, 2, 0):
        copy = remote(
            perm_in.at[m, 0, mine], wanted.at[pl.ds(m * part, part)], req_send.at[m], req_recv.at[m], {"dom": partners[m]}
        )
        copy.start()
        requests[m] = copy
    for copy in got_weights:
        copy.wait()
    w_copies = []
    for k, dev in enumerate(others):
        copy = remote(weights.at[head], weights.at[head], w_send.at[k], w_recv.at[head], {"head": dev})
        copy.start()
        w_copies.append(copy)

    got_rest = [
        fetch(6, wo_in, wo),
        fetch(7, gains_in, gains),
        fetch(8, vtab_in, vtab),
        fetch(9, mask_in.at[mine], mask),
        fetch(10, vids_in.at[:, mine], vids),
    ]
    got_links = [
        fetch(11 + e, links_in.at[e, mine], links.at[pl.ds(e * part, part)]) for e in range(link_count)
    ]

    got_feats.wait()
    widen(feats, 0, table, 0, nodes)

    sent = []

    used = [0]

    def send_chunk(rows, index, first, dst, send, recv, device):
        to = packed.at[pl.ds(used[0], rows)]
        used[0] += rows
        gather_rows(rows, index, first, table, staged, 0)
        to[...] = staged[0:rows, :].astype(BF16)
        copy = remote(to, dst, send, recv, device)
        copy.start()
        sent.append(copy)
        return copy

    def shared(base, h):
        return lists.at[pl.ds(pl.multiple_of(base * halo + direct + h * share, 128), share)]

    for copy in got_first:
        copy.wait()
    to_side = {"dom": side}
    quarter = send_chunk(
        share, send_first, direct, shared(1 - core, head), list_send.at[0], list_recv.at[0], to_side
    )
    list_copies = []
    for i in range(direct // chunk):
        at = pl.multiple_of((1 - core) * halo + i * chunk, chunk)
        dst = lists.at[pl.ds(at, chunk)]
        s = 1 + i
        list_copies.append(
            send_chunk(chunk, send_first, i * chunk, dst, list_send.at[s], list_recv.at[s], to_side)
        )

    pieces = part // PIECE
    row_copies = {}

    def serve(m, i):
        if i == 0:
            requests[m].wait_recv()
        s = m * pieces + i
        row_copies[m, i] = send_chunk(
            PIECE,
            wanted,
            m * part + i * PIECE,
            matched.at[m, pl.ds(i * PIECE, PIECE)],
            rows_send.at[s],
            rows_recv.at[s],
            {"dom": partners[m]},
        )

    got_second.wait()
    for i in range(halo // chunk):
        at = pl.multiple_of(core * halo + i * chunk, chunk)
        dst = lists.at[pl.ds(at, chunk)]
        s = 1 + direct // chunk + i
        list_copies.append(
            send_chunk(
                chunk, send_second, i * chunk, dst, list_send.at[s], list_recv.at[s], {"dom": peer}
            )
        )

    quarter.wait_recv()
    passed = []
    for k, dev in enumerate(others):
        copy = remote(
            shared(core, head), shared(core, head), pass_send.at[k], pass_recv.at[head], {"head": dev}
        )
        copy.start()
        passed.append(copy)
    for i in range(pieces):
        serve(1, i)
        serve(2, i)
    for i in range(pieces):
        serve(0, i)

    for dev in others:
        remote(weights.at[head], weights.at[dev], w_send.at[0], w_recv.at[dev], {"head": dev}).wait_recv()
    for copy in got_rest:
        copy.wait()
    prepare(
        weights, wo, gains, vtab[...], feats[mine, :], wq_p, wkv_p, w1_t, w2_t, wo_t, gain_cols,
        q_rows, k_rows, q_t, own_t, v_t, vk_h, vv_h,
    )
    for b in range(part // BLOCK):
        near_block(b, mask, vids, q_rows, k_rows, vk_h, probs, hub_probs, near_top, near_sum)
    for b in range(part // BLOCK):
        near_values(b, probs, hub_probs, v_t, vv_h, near_out)

    for copy in list_copies:
        copy.wait_recv()
    from_peer = pl.multiple_of((1 - core) * halo, halo)
    from_side = pl.multiple_of(core * halo, halo)
    widen(lists, from_peer, table, from_peer, halo)
    widen(lists, from_side, table, from_side, direct)
    for dev in others:
        remote(
            shared(core, head), shared(core, dev), pass_send.at[0], pass_recv.at[dev], {"head": dev}
        ).wait_recv()
    passed_on = pl.multiple_of(core * halo + direct, chunk)
    widen(lists, passed_on, table, passed_on, halo - direct)
    for copy in got_links:
        copy.wait()
    for i in range(pieces):
        row_copies[0, i].wait_recv()
    row_refs = [(far, e * part) for e in range(link_count)] + [(matched.at[0], 0)]
    for c in range(part // 256):
        for e in range(link_count):
            gather_rows(256, links, e * part + c * 256, table, far, e * part + c * 256)
        far_chunk(c, 256, row_refs, wkv_p, q_t, near_out, near_top, near_sum)
    for m in (2, 1):
        for i in range(pieces):
            row_copies[m, i].wait_recv()
    row_refs = [(matched.at[m], 0) for m in (1, 2)]
    for c in range(part // 256):
        far_chunk(c, 256, row_refs, wkv_p, q_t, near_out, near_top, near_sum, attended)
    ffn_chunk(
        0,
        part,
        own_t,
        attended,
        wo_t,
        w1_t,
        w2_t,
        gain_cols,
        out,
    )
    for copy in list(requests.values()) + w_copies + sent + passed:
        copy.wait_send()


def per_device(
    features,
    qkv_weight,
    out_weight,
    ffn_in,
    ffn_out,
    norm_gains,
    virtual_table,
    block_mask,
    halo_send,
    halo_links,
    expander_perm,
    virtual_ids,
):
    nodes, width = features.shape
    n_dom = lax.axis_size("dom")
    n_head = lax.axis_size("head")
    part = nodes // n_head
    halo = halo_send.shape[2]
    heads = width // HEAD_DIM
    n_virt = virtual_table.shape[0]
    wqkv = jnp.transpose(qkv_weight, (1, 2, 0)).reshape(-1, width)
    w1 = ffn_in.T
    w_rows = wqkv.shape[0] + 2 * w1.shape[0]
    hidden = n_head * w1.shape[0]
    links = halo_links.T
    link_count = links.shape[0]
    vids = virtual_ids.reshape(1, nodes)
    chunk = CHUNK
    direct = halo // 4
    share = (halo - direct) // n_head
    lists = 1 + direct // chunk + halo // chunk
    pieces = 3 * part // PIECE
    i32 = jnp.int32
    dma = pltpu.SemaphoreType.DMA
    return pl.pallas_call(
        functools.partial(layer_kernel, n_dom, n_head),
        name="layer",
        out_shape=jax.ShapeDtypeStruct((part, width), BF16),
        in_specs=[pl.BlockSpec(memory_space=pl.ANY)] * 12,
        out_specs=pl.BlockSpec(memory_space=pltpu.VMEM),
        scratch_shapes=[
            pltpu.VMEM((nodes, width), BF16),
            pltpu.VMEM((nodes, width), F32),
            pltpu.VMEM((chunk, width), F32),
            pltpu.VMEM((share + direct + halo + 3 * part, width), BF16),
            pltpu.VMEM((n_head, w_rows, width), BF16),
            pltpu.VMEM((width, width), BF16),
            pltpu.VMEM((2, width), F32),
            pltpu.VMEM((n_virt, width), BF16),
            pltpu.VMEM((part, BLOCK), i32),
            pltpu.VMEM((1, part), i32),
            pltpu.SMEM((direct + share,), i32),
            pltpu.SMEM((halo,), i32),
            pltpu.SMEM((link_count * part,), i32),
            pltpu.SMEM((3 * part,), i32),
            pltpu.VMEM((2 * halo, width), BF16),
            pltpu.VMEM((3, part, width), BF16),
            pltpu.VMEM((link_count * part, width), F32),
            pltpu.VMEM((width, width), BF16),
            pltpu.VMEM((2 * width, width), BF16),
            pltpu.VMEM((hidden, width), BF16),
            pltpu.VMEM((width, hidden), BF16),
            pltpu.VMEM((width, width), BF16),
            pltpu.VMEM((2, width, width), F32),
            pltpu.VMEM((part, width), BF16),
            pltpu.VMEM((part, width), BF16),
            pltpu.VMEM((width, part), F32),
            pltpu.VMEM((width, part), F32),
            pltpu.VMEM((width, part), BF16),
            pltpu.VMEM((heads * n_virt, width), BF16),
            pltpu.VMEM((width, heads * n_virt), BF16),
            pltpu.VMEM((width, part), F32),
            pltpu.VMEM((heads, part), F32),
            pltpu.VMEM((heads, part), F32),
            pltpu.VMEM((width, part), BF16),
            pltpu.VMEM((heads * part, BLOCK), BF16),
            pltpu.VMEM((heads * n_virt * part // BLOCK, BLOCK), F32),
            dma((12 + link_count,)),
            dma((3,)),
            dma((3,)),
            dma((lists,)),
            dma((lists,)),
            dma((pieces,)),
            dma((pieces,)),
            dma((n_head - 1,)),
            dma((n_head,)),
            dma((n_head - 1,)),
            dma((n_head,)),
        ],
        compiler_params=pltpu.CompilerParams(
            collective_id=0, has_side_effects=True, vmem_limit_bytes=60 << 20
        ),
    )(
        features,
        wqkv,
        out_weight,
        w1,
        ffn_out,
        norm_gains,
        virtual_table,
        block_mask,
        halo_send,
        links,
        expander_perm,
        vids,
    )


def solution(mesh):
    return jax.shard_map(
        per_device,
        mesh=mesh,
        in_specs=(
            P("dom", None),
            P(None, None, "head"),
            P(),
            P(None, "head"),
            P("head", None),
            P(),
            P(),
            P("dom", None),
            P("dom", None, None),
            P("dom", None),
            P(None, "dom", None),
            P("dom"),
        ),
        out_specs=P(("dom", "head"), None),
        check_vma=False,
    )
```
